32 devices in a mesh: cells: 2 (over x), pencil: 16 (over z, y, core).
Axes of the slice: x: 2, y: 2, z: 4, core: 2. Of those that a mesh axis runs over, the one named last changes fastest.
Arguments:
- multipoles: float32 [81, 128], P(None, ('cells', 'pencil')), parts along dimension 1, may hold values from -0.3 to 0.3
- positions: float32 [3, 128], P(None, ('cells', 'pencil')), parts along dimension 1, may hold values from 0 to 1
- species: int32 [128], P(('cells', 'pencil')), parts along dimension 0, may hold values from 0 to 2
- atom_slot: int32 [128], P('cells'), parts along dimension 0, may hold values from 0 to 63, each once
- pseudo_radial: float32 [3, 9, 262144], P(None, None, ('cells', 'pencil')), parts along dimension 2, may hold values from -1 to 1
- boundary_bessel: float32 [3, 9, 262144], P(None, None, ('cells', 'pencil')), parts along dimension 2, may hold values from -1 to 1
- interstitial: float32 [2, 262144], P(None, ('cells', 'pencil')), parts along dimension 1, may hold values from -6 to 6
- g_index: int32 [262144], P(('cells', 'pencil')), parts along dimension 0, may hold values from 0 to 1048575, as said below
Outputs:
- potential: float32 [512, 256, 256], P('cells', 'pencil'), parts along dimension 0
- boundary: float32 [81, 128], P(None, ('cells', 'pencil')), parts along dimension 1
The draws below stay inside these ranges and needn't reach their ends.
There are 2 independent parts, one for each index of `cells`. The reference program is written for one: setup_inputs(seed, part) draws one part's arguments, and reference() takes and returns one part's arrays. A program takes and returns all parts, laid end to end along the dimension named above; each array names one. Nothing has to cross between parts.
Inputs may be any that keep to these rules, and one draw needn't show every extreme that they name: `g_index`: each block of 8192 entries belongs to one pencil index and holds distinct positions v of that index's 16 planes: plane v // 65536, row (v // 256) % 256, column v % 256. atom_slot is a permutation of the atoms. Atom a's inputs (multipoles, positions, species) are held by pencil index a // 4; its boundary values go to column atom_slot[a], which is held by pencil index atom_slot[a] // 4.
All inputs are finite; a program needn't handle non-finite values.
Results may differ from the reference program's by a relative error of at most 0.0003.
Values sent between devices are 32-bit elements; how exact they have to be, the bound alone decides.
No kernel may reach another device: no remote copies, remote signals or barrier semaphores. Data moves between devices by JAX's collectives and lax.ppermute only.
A program may use at most 128 MiB of HBM per device.

```python
import math
import jax
import jax.numpy as jnp
import numpy as np
from jax import lax

NG = 256
LMAX = 8
SPECIES = 3
G_DEV = 8192
LM = 81
PLANES = 16
ATOMS = 64
G_TOTAL = 131072
N_PENCIL = 16


def draw_g_index(key, part):
    key = jax.random.fold_in(key, 7)
    blocks = G_TOTAL // G_DEV
    span = PLANES * NG * NG
    block_keys = jax.random.split(key, blocks)
    chosen = jax.random.randint(jax.random.fold_in(key, 1), (), 0, blocks)

    def one_block(block_key, number):
        scores = jax.random.randint(block_key, (span,), 0, 1073741824)
        last_slot = jnp.arange(span) == span - 1
        scores = jnp.where(last_slot & (number == chosen), -1, scores)
        return jnp.argsort(scores, stable=True)[:G_DEV].astype(jnp.int32)
    return jax.vmap(one_block)(block_keys, jnp.arange(blocks)).reshape(-1)


def set_ends(values, own_key, low, largest):
    extent = values.shape
    index_at = [jax.random.randint(jax.random.fold_in(own_key, axis), (), 0, extent[axis]) for axis in range(len(extent))]
    values = values.at[tuple(index_at)].set(low)
    longest = extent.index(max(extent))
    index_at[longest] = (index_at[longest] + 1) % extent[longest]
    return values.at[tuple(index_at)].set(largest)


def levels(stream_key, extent, shards, smallest, largest):
    factor_of, own = 1.0, jax.random.fold_in(stream_key, 6)
    for position, shards_of in shards:
        steps = jnp.exp(jax.random.uniform(jax.random.fold_in(own, position), (shards_of,), jnp.float32, smallest / len(shards), largest / len(shards)))
        factor_of = factor_of * jnp.repeat(steps, extent[position] // shards_of).reshape([-1 if axis == position else 1 for axis in range(len(extent))])
    return factor_of


def scatter_about(stream_key, shape, scale, most, shards=(), kind=jnp.bfloat16):
    gain = levels(stream_key, shape, shards, -0.22, 0.18) if shards else 1.0
    values = jax.random.normal(stream_key, shape, jnp.float32) * scale * gain
    return jnp.minimum(jnp.maximum(values, -most), most).astype(kind)


def setup_inputs(seed: int = 0, part: int = 0) -> dict:
    keys = jax.random.split(jax.random.key(seed), 9)
    part_splits = jax.random.split(jax.random.fold_in(keys[8], part), 9)
    return {
        "multipoles": scatter_about(part_splits[0], (LM, ATOMS), 0.05, 0.3, ((1, 16),), jnp.float32),
        "positions": jnp.clip(1.0 * jax.random.uniform(part_splits[1], (3, ATOMS), jnp.float32) ** levels(part_splits[1], (3, ATOMS), ((1, 16),), -0.2, 0.2), 0.0, 1.0),
        "species": set_ends(jax.random.randint(part_splits[2], (ATOMS,), 0, SPECIES), jax.random.fold_in(part_splits[2], 1), 0, SPECIES - 1).astype(jnp.int32),
        "atom_slot": jax.random.permutation(part_splits[3], ATOMS).astype(jnp.int32),
        "pseudo_radial": jnp.clip(jax.random.uniform(part_splits[4], (SPECIES, LMAX + 1, G_TOTAL), jnp.float32, -1.0, 1.0) * levels(part_splits[4], (SPECIES, LMAX + 1, G_TOTAL), ((2, 16),), -0.4, 0.0), -1.0, 1.0),
        "boundary_bessel": jnp.clip(jax.random.uniform(part_splits[5], (SPECIES, LMAX + 1, G_TOTAL), jnp.float32, -1.0, 1.0) * levels(part_splits[5], (SPECIES, LMAX + 1, G_TOTAL), ((2, 16),), -0.4, 0.0), -1.0, 1.0),
        "interstitial": scatter_about(part_splits[6], (2, G_TOTAL), 1.0, 6.0, ((1, 16),), jnp.float32),
        "g_index": draw_g_index(jax.random.fold_in(jax.random.fold_in(keys[8], part), 71), part),
    }


HIGH = lax.Precision.HIGHEST
TWO_PI = 2.0 * math.pi

def harmonics(freq_x, freq_y, freq_z):
    size_sq = freq_x * freq_x + freq_y * freq_y + freq_z * freq_z
    inv_size = 1.0 / jnp.sqrt(jnp.maximum(size_sq, 1.0))
    unit_x = freq_x * inv_size
    unit_y = freq_y * inv_size
    unit_z = freq_z * inv_size
    radius_sq = unit_x * unit_x + unit_y * unit_y + unit_z * unit_z
    all_ones = jnp.ones_like(unit_x)
    cosines = [all_ones]
    sine_terms = [jnp.zeros_like(unit_x)]
    for m_order in range(1, LMAX + 1):
        cosines.append(cosines[-1] * unit_x - sine_terms[-1] * unit_y)
        sine_terms.append(sine_terms[-1] * unit_x + cosines[-2] * unit_y)
    harm_rows = [None] * ((LMAX + 1) * (LMAX + 1))
    for m_order in range(LMAX + 1):
        start_value = float(np.prod(np.arange(1, 2 * m_order, 2)))
        before = None
        current = start_value * all_ones
        for degree in range(m_order, LMAX + 1):
            if degree == m_order + 1:
                before, current = (current, (2 * m_order + 1) * unit_z * current)
            elif degree > m_order + 1:
                before, current = (current, ((2 * degree - 1) * unit_z * current - (degree + m_order - 1) * radius_sq * before) / (degree - m_order))
            factor = math.sqrt((2 * degree + 1) / (4 * math.pi) * math.factorial(degree - m_order) / math.factorial(degree + m_order))
            centre = degree * degree + degree
            if m_order == 0:
                harm_rows[centre] = factor * current
            else:
                harm_rows[centre + m_order] = math.sqrt(2.0) * factor * current * cosines[m_order]
                harm_rows[centre - m_order] = math.sqrt(2.0) * factor * current * sine_terms[m_order]
    return jnp.stack(harm_rows)

def degree_counts():
    return 2 * np.arange(LMAX + 1) + 1

def settle(by_real, by_imag, species_pick):
    kinds = species_pick.shape[1]
    real_sel = lax.optimization_barrier(jnp.sum(by_real.reshape(-1, kinds, LM) * species_pick[:, :, None], axis=1))
    imag_sel = lax.optimization_barrier(jnp.sum(by_imag.reshape(-1, kinds, LM) * species_pick[:, :, None], axis=1))
    degrees = np.repeat(np.arange(LMAX + 1), degree_counts())
    even_rows = degrees % 2 == 0
    signs = np.where((degrees % 4 == 1) | (degrees % 4 == 2), -1.0, 1.0).astype(np.float32)
    return jnp.where(even_rows[None, :], real_sel, imag_sel) * signs[None, :]

def signed(index):
    return jnp.where(index >= NG // 2, index - NG, index).astype(jnp.float32)

def reference(multipoles, positions, species, atom_slot, pseudo_radial, boundary_bessel, interstitial, g_index):
    owner = jnp.arange(g_index.shape[0], dtype=jnp.int32) // G_DEV
    x_index = g_index // (NG * NG) * N_PENCIL + owner
    y_index = g_index // NG % NG
    z_index = g_index % NG
    freq_x = signed(x_index)
    freq_y = signed(y_index)
    freq_z = signed(z_index)
    counts = degree_counts()
    species_pick = (species[:, None] == jnp.arange(SPECIES, dtype=jnp.int32)[None, :]).astype(jnp.float32)
    weights = (species_pick.T[:, None, :] * multipoles[None]).reshape(SPECIES * LM, -1)
    starts = jnp.arange(N_PENCIL, dtype=jnp.int32) * G_DEV

    def block_geometry(start):
        block_x = lax.dynamic_slice_in_dim(freq_x, start, G_DEV)
        block_y = lax.dynamic_slice_in_dim(freq_y, start, G_DEV)
        block_z = lax.dynamic_slice_in_dim(freq_z, start, G_DEV)
        harm = harmonics(block_x, block_y, block_z)
        angle = TWO_PI * (positions[0][:, None] * block_x[None, :] + positions[1][:, None] * block_y[None, :] + positions[2][:, None] * block_z[None, :])
        return (harm, jnp.cos(angle), jnp.sin(angle))

    def charge_block(start):
        harm, cosine, sine = block_geometry(start)
        radial = lax.dynamic_slice_in_dim(pseudo_radial, start, G_DEV, 2)
        table = (jnp.repeat(radial, counts, axis=1, total_repeat_length=LM) * harm[None]).reshape(SPECIES * LM, G_DEV)
        shape_part = lax.dot_general(weights, table, (((0,), (0,)), ((), ())), precision=HIGH, preferred_element_type=jnp.float32)
        return (lax.optimization_barrier(jnp.sum(shape_part * cosine, axis=0)), -lax.optimization_barrier(jnp.sum(shape_part * sine, axis=0)))
    pseudo_re, pseudo_im = lax.map(charge_block, starts)
    rho_re = interstitial[0] + pseudo_re.reshape(-1)
    rho_im = interstitial[1] + pseudo_im.reshape(-1)
    size_sq = freq_x * freq_x + freq_y * freq_y + freq_z * freq_z
    kernel = jnp.where(size_sq > 0, 1.0 / jnp.maximum(size_sq, 1.0), 0.0)
    pot_re = rho_re * kernel
    pot_im = rho_im * kernel
    values = lax.complex(pot_re, pot_im)
    spectrum = jnp.zeros((NG, NG, NG), values.dtype).at[x_index, y_index, z_index].set(values)
    potential = jnp.real(jnp.fft.ifftn(spectrum)) * float(NG) ** 3

    def boundary_block(start):
        harm, cosine, sine = block_geometry(start)
        bessel = lax.dynamic_slice_in_dim(boundary_bessel, start, G_DEV, 2)
        table = (jnp.repeat(bessel, counts, axis=1, total_repeat_length=LM) * harm[None]).reshape(SPECIES * LM, G_DEV)
        part_re = lax.dynamic_slice_in_dim(pot_re, start, G_DEV)
        part_im = lax.dynamic_slice_in_dim(pot_im, start, G_DEV)
        real_part = part_re[None, :] * cosine - part_im[None, :] * sine
        imag_part = part_re[None, :] * sine + part_im[None, :] * cosine
        dims = (((1,), (1,)), ((), ()))
        return (lax.dot_general(real_part, table, dims, precision=HIGH, preferred_element_type=jnp.float32), lax.dot_general(imag_part, table, dims, precision=HIGH, preferred_element_type=jnp.float32))
    by_real, by_imag = lax.map(boundary_block, starts)
    combined = settle(lax.optimization_barrier(jnp.sum(by_real, axis=0)), lax.optimization_barrier(jnp.sum(by_imag, axis=0)), species_pick)
    boundary = jnp.zeros((LM, combined.shape[0]), combined.dtype).at[:, atom_slot].set(combined.T)
    return (potential.astype(jnp.float32), boundary)
```

```python
import functools
import math

import jax
import jax.numpy as jnp
import numpy as np
from jax import lax
from jax.experimental import pallas as pl
from jax.experimental.pallas import tpu as pltpu
from jax.sharding import PartitionSpec as P

NG = 256
LMAX = 8
LM = 81
KINDS = 3
ROWS = 256
CHUNK = 1024
HIGH = lax.Precision.HIGHEST
TWO_PI = 2.0 * math.pi
F32 = jnp.float32
BF16 = jnp.bfloat16
I32 = jnp.int32
VMEM_BYTES = 56 * 1024 * 1024


def norm(degree, m_order):
    base = (
        (2 * degree + 1)
        / (4 * math.pi)
        * math.factorial(degree - m_order)
        / math.factorial(degree + m_order)
    )
    return math.sqrt(base) * (math.sqrt(2.0) if m_order else 1.0)


def table_layout():
    tile_rows = [(d, 0) for d in range(1, 9)]
    tile_rows += [(8, m) for m in range(1, 9)] + [(8, -m) for m in range(1, 9)]
    tile_rows += [(4, r + 1) if r < 4 else (4, -(8 - r)) for r in range(8)]
    for low in (1, 2, 3):
        for sign in (1, -1):
            tile_rows += [
                (low, sign * (r + 1)) if r < low else (8 - low, sign * (8 - r)) for r in range(8)
            ]
    rows = {}
    for kind in range(KINDS):
        for at, (degree, m_order) in enumerate(tile_rows):
            rows[kind * 88 + at] = (kind, degree, m_order)
    rows[80] = (0, 0, 0)
    rows[168] = (1, 0, 0)
    rows[81] = (2, 0, 0)
    return rows


def placement_tables():
    spread = np.zeros((KINDS, 128, ROWS), np.float32)
    even = np.zeros((KINDS, ROWS, 128), np.float32)
    odd = np.zeros((KINDS, ROWS, 128), np.float32)
    for row, (kind, degree, m_order) in table_layout().items():
        lm = degree * degree + degree + m_order
        spread[kind, lm, row] = 1.0
        sign = -1.0 if degree % 4 in (1, 2) else 1.0
        (even if degree % 2 == 0 else odd)[kind, row, lm] = sign
    return spread, np.concatenate([even, odd], 0)


def recurrence_table():
    out = np.zeros((8, 128), np.float64)
    for direction in range(2):
        for r in range(8):
            m = r + 1 if direction == 0 else 8 - r
            start = float(np.prod(np.arange(1, 2 * m, 2)))
            for degree in range(1, 9):
                at = 3 * (8 * direction + degree - 1)
                if degree == m:
                    out[r, at + 2] = start * norm(m, m)
                elif degree > m:
                    out[r, at] = (
                        (2 * degree - 1) / (degree - m) * norm(degree, m) / norm(degree - 1, m)
                    )
                    if degree > m + 1:
                        out[r, at + 1] = (
                            (degree + m - 1) / (degree - m) * norm(degree, m) / norm(degree - 2, m)
                        )
    return out.astype(np.float32)


def fit_even(values, count):
    x = np.cos(np.pi * (np.arange(400) + 0.5) / 400) * 0.125 + 0.125
    basis = np.polynomial.chebyshev.Chebyshev.fit(x, values(np.sqrt(x)), count - 1, domain=[0, 0.25])
    return [float(c) for c in basis.convert(kind=np.polynomial.Polynomial, domain=[-1, 1]).coef]


SIN_FIT = fit_even(lambda x: np.sin(np.pi * x) / x, 5)
COS_FIT = fit_even(lambda x: np.cos(np.pi * x), 5)


def horner(coefficients, x):
    total = coefficients[-1]
    for coefficient in coefficients[-2::-1]:
        total = total * x + coefficient
    return total


def turn(t):
    t = t - jnp.floor(t + 0.5)
    square = t * t
    half_sin = t * horner(SIN_FIT, square)
    half_cos = horner(COS_FIT, square)
    return 1.0 - 2.0 * half_sin * half_sin, 2.0 * half_sin * half_cos


def split(x):
    high = x.astype(BF16)
    return high, (x - high.astype(F32)).astype(BF16)


def signed(index):
    return jnp.where(index >= NG // 2, index - NG, index).astype(F32)


def frequencies(position, owner, count):
    jx = (position >> 16) * count + owner
    jy = (position >> 8) & 255
    jz = position & 255
    return jx, signed(jx), signed(jy), signed(jz)


def table_of(freq, radial_ref, coef_ref, rows_scratch):
    freq_x, freq_y, freq_z = freq
    size_sq = freq_x * freq_x + freq_y * freq_y + freq_z * freq_z
    inv_size = 1.0 / jnp.sqrt(jnp.maximum(size_sq, 1.0))
    unit_x, unit_y, unit_z = freq_x * inv_size, freq_y * inv_size, freq_z * inv_size
    radius_sq = unit_x * unit_x + unit_y * unit_y + unit_z * unit_z
    width = unit_x.shape[1]
    cosine, sine = unit_x, unit_y
    for m in range(1, 9):
        rows_scratch[0, m - 1 : m, :] = cosine
        rows_scratch[1, m - 1 : m, :] = sine
        rows_scratch[2, 8 - m : 9 - m, :] = cosine
        rows_scratch[3, 8 - m : 9 - m, :] = sine
        cosine, sine = cosine * unit_x - sine * unit_y, sine * unit_x + cosine * unit_y
    before, current = jnp.zeros_like(unit_z), jnp.ones_like(unit_z)
    for degree in range(1, 9):
        before, current = (
            current,
            (2 * degree - 1) / degree * unit_z * current
            - (degree - 1) / degree * radius_sq * before,
        )
        rows_scratch[4, degree - 1 : degree, :] = norm(degree, 0) * current
    wide_z = jnp.broadcast_to(unit_z, (8, width))
    wide_sq = jnp.broadcast_to(radius_sq, (8, width))
    plain = []
    for direction in range(2):
        before = jnp.zeros((8, width), F32)
        current = jnp.zeros((8, width), F32)
        by_degree = [None]
        for degree in range(1, 9 - direction):
            at = 3 * (8 * direction + degree - 1)
            following = coef_ref[:, at + 2 : at + 3] + (coef_ref[:, at : at + 1] * wide_z) * current
            if degree > 2:
                following = following - (coef_ref[:, at + 1 : at + 2] * wide_sq) * before
            before, current = current, following
            by_degree.append(current)
        plain.append(by_degree)
    forward, reverse = plain
    cos_f, sin_f, cos_r, sin_r = (rows_scratch[i] for i in range(4))
    sub = lax.broadcasted_iota(I32, (8, width), 0)
    harm = [rows_scratch[4], forward[8] * cos_f, forward[8] * sin_f]
    harm.append(jnp.where(sub < 4, forward[4] * cos_f, reverse[4] * sin_r))
    for low in (1, 2, 3):
        harm.append(jnp.where(sub < low, forward[low] * cos_f, reverse[8 - low] * cos_r))
        harm.append(jnp.where(sub < low, forward[low] * sin_f, reverse[8 - low] * sin_r))
    zeros = jnp.zeros((8, width), F32)
    pieces = []
    first = norm(0, 0)
    for kind in range(KINDS):
        line = [
            jnp.broadcast_to(radial_ref[d, kind : kind + 1, :], (8, width)) for d in range(1, 9)
        ]
        line = [None] + line
        for d in range(1, 9):
            rows_scratch[5 + kind, d - 1 : d, :] = radial_ref[d, kind : kind + 1, :]
        pieces.append(harm[0] * rows_scratch[5 + kind])
        pieces.append(harm[1] * line[8])
        pieces.append(harm[2] * line[8])
        pieces.append(harm[3] * line[4])
        for low in (1, 2, 3):
            both = jnp.where(sub < low, line[low], line[8 - low])
            pieces.append(harm[2 + 2 * low] * both)
            pieces.append(harm[3 + 2 * low] * both)
        if kind < 2:
            own = jnp.broadcast_to(radial_ref[0, kind : kind + 1, :], (8, width)) * first
            extra = jnp.where(sub == 0, own, zeros)
            if kind == 0:
                third = jnp.broadcast_to(radial_ref[0, 2:3, :], (8, width)) * first
                extra = jnp.where(sub == 1, third, extra)
            pieces.append(extra)
    return split(jnp.concatenate(pieces, 0))


def angles(atoms_ref, freq):
    freq_x, freq_y, freq_z = freq
    return turn(
        atoms_ref[:, LM : LM + 1] * freq_x
        + atoms_ref[:, LM + 1 : LM + 2] * freq_y
        + atoms_ref[:, LM + 2 : LM + 3] * freq_z
    )


def charge_kernel(
    count,
    place_ref,
    atoms_ref,
    spread_ref,
    coef_ref,
    radial_ref,
    inter_ref,
    index_ref,
    key_ref,
    order_ref,
    pot_ref,
    sent_ref,
    weights,
    rows_scratch,
    values,
):
    step = pl.program_id(0)
    atoms = atoms_ref.shape[0]
    per_chunk = CHUNK // 128

    @pl.when(step == 0)
    def _():
        kind = atoms_ref[:, LM + 3 : LM + 4]
        total = jnp.zeros((atoms, ROWS), F32)
        for s in range(KINDS):
            moved = jnp.dot(
                atoms_ref[...], spread_ref[s], precision=HIGH, preferred_element_type=F32
            )
            total = total + jnp.where(kind == float(s), moved, 0.0)
        high, low = split(total)
        weights[0:atoms, :] = high
        weights[atoms : 2 * atoms, :] = low

    jx, *freq = frequencies(index_ref[...], place_ref[0], count)
    table_high, table_low = table_of(freq, radial_ref, coef_ref, rows_scratch)
    main = jnp.dot(weights[...], table_high, preferred_element_type=F32)
    rest = jnp.dot(weights[0:atoms, :], table_low, preferred_element_type=F32)
    shape_part = main[0:atoms] + (main[atoms:] + rest)
    cosine, sine = angles(atoms_ref, freq)
    pseudo_re = jnp.sum(shape_part * cosine, axis=0, keepdims=True)
    pseudo_im = -jnp.sum(shape_part * sine, axis=0, keepdims=True)
    freq_x, freq_y, freq_z = freq
    size_sq = freq_x * freq_x + freq_y * freq_y + freq_z * freq_z
    kernel = jnp.where(size_sq > 0, 1.0 / jnp.maximum(size_sq, 1.0), 0.0)
    pot_re = (inter_ref[0:1, :] + pseudo_re) * kernel
    pot_im = (inter_ref[1:2, :] + pseudo_im) * kernel
    pot_ref[0:1, :] = pot_re
    pot_ref[1:2, :] = pot_im
    folded_im = jnp.where(jx > NG // 2, -pot_im, pot_im)
    for j in range(per_chunk):
        line = pl.ds(step * per_chunk + j, 1)
        values[0, line, :] = pot_re[:, j * 128 : (j + 1) * 128]
        values[1, line, :] = folded_im[:, j * 128 : (j + 1) * 128]

    @pl.when(step == pl.num_programs(0) - 1)
    def _():
        order = order_ref[...]
        lines = order.shape[0]
        lane = order & 127
        line_of = order >> 7

        def one_line(r, carried):
            taken_re, taken_im = carried
            here = line_of == r
            row_re = jnp.broadcast_to(values[0, pl.ds(r, 1), :], (lines, 128))
            row_im = jnp.broadcast_to(values[1, pl.ds(r, 1), :], (lines, 128))
            taken_re = jnp.where(here, jnp.take_along_axis(row_re, lane, axis=1), taken_re)
            taken_im = jnp.where(here, jnp.take_along_axis(row_im, lane, axis=1), taken_im)
            return taken_re, taken_im

        empty = jnp.zeros((lines, 128), F32)
        taken_re, taken_im = lax.fori_loop(0, lines, one_line, (empty, empty), unroll=8)
        key = key_ref[...]
        sent_ref[0:lines, :] = taken_re
        sent_ref[lines : 2 * lines, :] = taken_im
        sent_ref[2 * lines : 3 * lines, :] = key.astype(F32)
        at_lane = lax.broadcasted_iota(I32, (8, 128), 1)
        starts = jnp.zeros((8, 128), F32)
        for k in range(1, NG // count + 1):
            below = jnp.sum((key < (k << 16)).astype(F32), axis=(0, 1), keepdims=True)
            starts = jnp.where(at_lane == k, below, starts)
        sent_ref[3 * lines :, :] = starts


def boundary_kernel(
    count,
    place_ref,
    atoms_ref,
    gather_ref,
    coef_ref,
    slot_ref,
    bessel_ref,
    pot_ref,
    index_ref,
    out_ref,
    total,
    rows_scratch,
):
    step = pl.program_id(0)
    atoms = atoms_ref.shape[0]
    _, *freq = frequencies(index_ref[...], place_ref[0], count)
    table_high, table_low = table_of(freq, bessel_ref, coef_ref, rows_scratch)
    cosine, sine = angles(atoms_ref, freq)
    pot_re, pot_im = pot_ref[0:1, :], pot_ref[1:2, :]
    real_part = pot_re * cosine - pot_im * sine
    imag_part = pot_re * sine + pot_im * cosine
    high, low = split(jnp.concatenate([real_part, imag_part], 0))
    dims = (((1,), (1,)), ((), ()))
    both = lax.dot_general(
        jnp.concatenate([high, low], 0), table_high, dims, preferred_element_type=F32
    )
    rest = lax.dot_general(high, table_low, dims, preferred_element_type=F32)
    add = both[0 : 2 * atoms] + (both[2 * atoms :] + rest)

    @pl.when(step == 0)
    def _():
        total[...] = add

    @pl.when(step > 0)
    def _():
        total[...] += add

    @pl.when(step == pl.num_programs(0) - 1)
    def _():
        kind = atoms_ref[:, LM + 3 : LM + 4]
        raw = jnp.zeros((atoms, 128), F32)
        for s in range(KINDS):
            part = jnp.dot(
                total[0:atoms, :], gather_ref[s], precision=HIGH, preferred_element_type=F32
            ) + jnp.dot(
                total[atoms:, :], gather_ref[KINDS + s], precision=HIGH, preferred_element_type=F32
            )
            raw = raw + jnp.where(kind == float(s), part, 0.0)
        slots = lax.broadcasted_iota(I32, (atoms, atoms), 0)
        moved = (slots == slot_ref[...]).astype(F32)
        out_ref[...] = jnp.dot(moved, raw, precision=HIGH, preferred_element_type=F32)


def window_chunks(count, local_g):
    mean = local_g * count // NG
    return 2 * math.ceil((mean + 128 + 5 * math.sqrt(mean)) / 256)


def planes_kernel(count, pattern, finish, *refs):
    if finish:
        place_ref, start_ref, recv_ref, step_ref, wave_ref, before_ref, _ = refs[:7]
        own_ref, other_ref, box, front, back, spots, wave, earlier, sem = refs[7:]
    else:
        place_ref, start_ref, recv_ref, step_ref, box, front, back, spots = refs
    rows = NG // count
    planes = NG // count
    chip_rows = 2 * rows
    sources = recv_ref.shape[0]
    lines = (recv_ref.shape[1] - 8) // 3
    wide = window_chunks(count, lines * 128)
    half_planes = NG // 4
    per_plane = lines // planes
    place = place_ref[0]
    core = place % 2
    base = (place // 2) * chip_rows

    if finish and before_ref is not None:
        fetch = pltpu.make_async_copy(before_ref, earlier, sem)
        fetch.start()
    box[...] = jnp.zeros_like(box)
    for held in (front, back):
        held[lines:] = jnp.zeros((wide, 4 * chip_rows, 128), BF16)

    sub = lax.broadcasted_iota(I32, (8, 128), 0)
    if chip_rows == 8:
        start_rows = (base + (sub + core * rows) % chip_rows).astype(F32) * (1.0 / NG)
    else:
        start_rows = (base + core * rows + sub).astype(F32) * (1.0 / NG)
    across = (1 - 2 * core).astype(F32) * (rows / NG)

    def all_spots(s, _):
        keys = recv_ref[s, 2 * lines : 3 * lines, :].astype(I32)
        spots[s, 0:lines, :] = (((keys >> 16) << 8) | (keys & 255)).astype(F32)
        spots[s, lines:, :] = jnp.full((wide, 128), -1.0, F32)
        return 0

    lax.fori_loop(0, sources, all_spots, 0)

    def one_chunk(s, i, held):
        key = recv_ref[s, pl.ds(2 * lines + i, 1), :].astype(I32)
        v_re = recv_ref[s, pl.ds(i, 1), :]
        v_im = recv_ref[s, pl.ds(lines + i, 1), :]
        jy = ((key >> 8) & 255).astype(F32)
        wide_y = jnp.broadcast_to(jy, (8, 128))
        c, s = turn(wide_y * start_rows)
        parts = [(v_re * c - v_im * s, v_re * s + v_im * c)]
        if chip_rows > 8:
            c, s = turn(wide_y * (8.0 / NG))
            while 8 * len(parts) < rows:
                re, im = parts[-1]
                parts.append((re * c - im * s, re * s + im * c))
            c, s = turn(wide_y * across)
            parts += [(re * c - im * s, re * s + im * c) for re, im in parts]
        high, low = split(jnp.concatenate([re for re, _ in parts] + [im for _, im in parts], 0))
        held[i] = jnp.concatenate([high, low], 0)

    def start_of(s, k):
        return start_ref[s, 0, k].astype(I32)

    def one_window(s, k, first, held):
        left, right = [], []
        for j in range(wide):
            spot = spots[s, pl.ds(first + j, 1), :] - (k * NG).astype(F32)
            spot = jnp.broadcast_to(spot, (16, 128)).astype(BF16)
            hits = [
                jnp.where(
                    step_ref[16 * r : 16 * r + 16, :] == spot,
                    jnp.ones((16, 128), BF16),
                    jnp.zeros((16, 128), BF16),
                )
                for r in range(NG // 16)
            ]
            left.append(held[first + j])
            right.append(jnp.concatenate(hits, 0))
        out = lax.dot_general(
            jnp.concatenate(left, 1),
            jnp.concatenate(right, 1),
            (((1,), (1,)), ((), ())),
            preferred_element_type=F32,
        )
        owner = place ^ (4 * s + pattern) if pattern is not None else 2 * s + core
        jx = k * count + owner
        at = jnp.where(jx > NG // 2, NG - jx, jx) // 2
        box[at] += out[0 : 2 * chip_rows] + out[2 * chip_rows :]

    def one_source(s, held, following, filled):
        def one_plane(k, longest):
            first = start_of(s, k) // 128
            one_window(s, k, first, held)
            for j in range(per_plane):
                one_chunk(following, k * per_plane + j, filled)
            return jnp.maximum(longest, start_of(s, k + 1) - first * 128)

        unroll = 4 if planes % 4 == 0 and planes > 4 else 1
        longest = lax.fori_loop(0, planes, one_plane, jnp.int32(0), unroll=unroll)

        @pl.when(longest > wide * 128)
        def _():
            def long_plane(k, _):
                first = start_of(s, k) // 128
                more = (start_of(s, k + 1) - first * 128 + wide * 128 - 1) // (wide * 128)

                def again(j, _):
                    one_window(s, k, first + j * wide, held)
                    return 0

                return lax.fori_loop(1, more, again, 0)

            lax.fori_loop(0, planes, long_plane, 0)

    def first_chunks(g, _):
        for j in range(4):
            one_chunk(0, 4 * g + j, front)
        return 0

    lax.fori_loop(0, lines // 4, first_chunks, 0)

    def two_sources(t, _):
        one_source(2 * t, front, 2 * t + 1, back)
        one_source(2 * t + 1, back, jnp.minimum(2 * t + 2, sources - 1), front)
        return 0

    lax.fori_loop(0, sources // 2, two_sources, 0)
    if not finish:
        return

    wave[0], wave[1] = split(wave_ref[...])
    if before_ref is not None:
        fetch.wait()

    def along_z(at, number):
        size = number * 2 * chip_rows
        block = box[pl.ds(at, number)]
        if before_ref is not None:
            block = block + earlier[pl.ds(at, number)]
        high, low = split(block.reshape(size, NG))
        main = jnp.dot(jnp.concatenate([high, low], 0), wave[0], preferred_element_type=F32)
        rest = jnp.dot(high, wave[1], preferred_element_type=F32)
        full = (main[:size] + (main[size:] + rest)).reshape(number, 2 * chip_rows, 2 * NG)
        re, im = full[:, :chip_rows], full[:, chip_rows:]
        return re[:, :, :NG] - im[:, :, NG:], re[:, :, NG:] + im[:, :, :NG]

    def keep(at, value):
        line = pl.ds(at, rows, stride=NG // 2)
        for h in range(2):
            own_ref[h, line, :] = value[:rows, h * 128 : (h + 1) * 128]
            other_ref[h, line, :] = value[rows:, h * 128 : (h + 1) * 128]

    group = 4

    def some_planes(g, _):
        re, im = along_z(g * group, group)
        for j in range(group):
            keep(2 * (g * group + j), re[j])
            keep(2 * (g * group + j) + 1, im[j])
        return 0

    lax.fori_loop(0, half_planes // group, some_planes, 0, unroll=2)

    @pl.when(core == 0)
    def _():
        re, _ = along_z(half_planes, 1)
        keep(1, re[0])


def planes_call(count, place, recv, pattern, steps, finish=False, wave=None, before=None, after=None):
    rows = NG // count
    sources = recv.shape[0]
    lines = (recv.shape[1] - 8) // 3
    wide = window_chunks(count, lines * 128)
    half_rows = rows * NG // 2
    box = (NG // 4 + 1, 4 * rows, NG)
    vmem = pl.BlockSpec(memory_space=pltpu.VMEM)
    held = pltpu.VMEM((lines + wide, 8 * rows, 128), BF16)
    scratch = [held, held, pltpu.VMEM((sources, lines + wide, 128), F32)]
    start_spec = pl.BlockSpec(
        (sources, 8, 128), lambda i: (0, 3 * lines // 8, 0), memory_space=pltpu.SMEM
    )
    recv_spec = pl.BlockSpec(recv.shape, lambda i: (0, 0, 0))
    step_spec = pl.BlockSpec(steps.shape, lambda i: (0, 0))
    in_specs = [smem(), start_spec, recv_spec, step_spec]
    operands = [place, recv, recv, steps]
    kernel = functools.partial(planes_kernel, count, pattern, finish)
    if not finish:
        return pl.pallas_call(
            kernel,
            grid=(1,),
            in_specs=in_specs,
            out_specs=pl.BlockSpec(box, lambda i: (0, 0, 0)),
            out_shape=jax.ShapeDtypeStruct(box, F32),
            scratch_shapes=scratch,
            compiler_params=params(),
            name="planes_near",
        )(*operands)
    scratch = [pltpu.VMEM(box, F32)] + scratch + [pltpu.VMEM((2, NG, 2 * NG), BF16)]
    anywhere = pl.BlockSpec(memory_space=pl.ANY)
    in_specs.append(pl.BlockSpec(wave.shape, lambda i: (0, 0)))
    operands.append(wave)
    if before is None:
        inner = kernel
        at = len(in_specs)

        def kernel(*refs):
            inner(*refs[:at], None, *refs[at:], None, None)

    else:
        in_specs.append(anywhere)
        operands.append(before)
        scratch += [pltpu.VMEM(box, F32), pltpu.SemaphoreType.DMA]
    in_specs.append(anywhere)
    operands.append(after)
    return pl.pallas_call(
        kernel,
        grid=(1,),
        in_specs=in_specs,
        out_specs=[pl.BlockSpec((2, half_rows, 128), lambda i: (0, 0, 0))] * 2,
        out_shape=[jax.ShapeDtypeStruct((2, half_rows, 128), F32)] * 2,
        scratch_shapes=scratch,
        compiler_params=params(),
        name="planes",
    )(*operands)


def last_kernel(count, place_ref, own_ref, other_ref, wave_ref, _, out_ref, held, wave, sem):
    rows = NG // count
    half = NG // 2
    wave[0], wave[1] = split(wave_ref[place_ref[0] % 2])

    def one_row(y, _):
        line = pl.ds(pl.multiple_of(y * half, half), half)
        mixed = [
            jnp.concatenate([own_ref[h, line, :], other_ref[h, line, :]], 0) for h in range(2)
        ]
        high, low = split(jnp.concatenate(mixed, 1))
        main = jnp.dot(wave[...].reshape(2 * NG, NG), high, preferred_element_type=F32)
        rest = jnp.dot(wave[0], low, preferred_element_type=F32)
        out = main[:NG] + (main[NG:] + rest)
        for h in range(2):
            held[h, pl.ds(y, NG, stride=rows), :] = out[:, h * 128 : (h + 1) * 128]
        return 0

    lax.fori_loop(0, rows, one_row, 0, unroll=4)
    copies = [
        pltpu.make_async_copy(held.at[h], out_ref.at[:, pl.ds(h * 128, 128)], sem.at[h])
        for h in range(2)
    ]
    for copy in copies:
        copy.start()
    for copy in copies:
        copy.wait()


def wave_tables():
    j = np.arange(NG)
    phase = 2 * np.pi / NG * ((j[:, None] * j[None, :]) % NG)
    along_z = np.concatenate([np.cos(phase), np.sin(phase)], 1)
    classes = []
    for core in range(2):
        table = np.zeros((NG, NG // 2))
        for i in range(NG // 4):
            phase_x = 2 * np.pi / NG * ((j * (2 * i + core)) % NG)
            table[:, 2 * i] = np.cos(phase_x)
            table[:, 2 * i + 1] = -np.sin(phase_x)
        if core == 0:
            table[:, 1] = np.cos(np.pi * j)
        classes.append(table)
    along_x = [np.concatenate([classes[c], classes[1 - c]], 1) for c in range(2)]
    return along_z.astype(np.float32), np.stack(along_x).astype(np.float32)


def smem():
    return pl.BlockSpec(memory_space=pltpu.SMEM)


def params():
    return pltpu.CompilerParams(vmem_limit_bytes=VMEM_BYTES)


def body(
    multipoles, positions, species, atom_slot, pseudo_radial, boundary_bessel, interstitial, g_index
):
    count = lax.axis_size("pencil")
    owner = lax.axis_index("pencil").astype(I32)
    place = owner.reshape(1)
    local_g = g_index.shape[0]
    lines = local_g // 128
    chunks = local_g // CHUNK
    atoms = atom_slot.shape[0]
    own_atoms = multipoles.shape[1]
    rows = NG // count
    spread, gather = placement_tables()
    coef = jnp.asarray(recurrence_table())
    along_z, along_x = wave_tables()

    mine = jnp.concatenate(
        [multipoles, positions, species.astype(F32)[None, :], jnp.zeros((43, own_atoms), F32)], 0
    ).T
    copies = jnp.broadcast_to(mine[None], (count, own_atoms, 128))
    atom_rows = lax.all_to_all(copies, "pencil", split_axis=0, concat_axis=0, tiled=True)
    atom_rows = atom_rows.reshape(atoms, 128)

    jx = (g_index >> 16) * count + owner
    flip = jx > NG // 2
    jy = (g_index >> 8) & 255
    jz = g_index & 255
    folded = jnp.where(flip, ((-jy & 255) << 8) | (-jz & 255), (jy << 8) | jz)
    key, order = lax.sort(
        (((g_index >> 16) << 16) | folded, lax.iota(I32, local_g)), num_keys=1, is_stable=False
    )
    key = key.reshape(lines, 128)
    order = order.reshape(lines, 128)
    index_line = g_index.reshape(1, local_g)

    whole = lambda a: pl.BlockSpec(a.shape, lambda i: (0,) * a.ndim)
    line_spec = pl.BlockSpec((1, CHUNK), lambda i: (0, i))
    pair_spec = pl.BlockSpec((2, CHUNK), lambda i: (0, i))
    radial_spec = pl.BlockSpec((LMAX + 1, KINDS, CHUNK), lambda i: (0, 0, i))
    spread = jnp.asarray(spread)
    pot, sent = pl.pallas_call(
        functools.partial(charge_kernel, count),
        grid=(chunks,),
        in_specs=[
            smem(),
            whole(atom_rows),
            whole(spread),
            whole(coef),
            radial_spec,
            pair_spec,
            line_spec,
            whole(key),
            whole(order),
        ],
        out_specs=[pair_spec, pl.BlockSpec((3 * lines + 8, 128), lambda i: (0, 0))],
        out_shape=[
            jax.ShapeDtypeStruct((2, local_g), F32),
            jax.ShapeDtypeStruct((3 * lines + 8, 128), F32),
        ],
        scratch_shapes=[
            pltpu.VMEM((2 * atoms, ROWS), BF16),
            pltpu.VMEM((8, 8, CHUNK), F32),
            pltpu.VMEM((2, lines, 128), F32),
        ],
        compiler_params=params(),
        name="charge",
    )(place, atom_rows, spread, coef, pseudo_radial.transpose(1, 0, 2), interstitial, index_line, key, order)

    gather = jnp.asarray(gather)
    slot_line = atom_slot.reshape(1, atoms)
    partial_raw = pl.pallas_call(
        functools.partial(boundary_kernel, count),
        grid=(chunks,),
        in_specs=[
            smem(),
            whole(atom_rows),
            whole(gather),
            whole(coef),
            whole(slot_line),
            radial_spec,
            pair_spec,
            line_spec,
        ],
        out_specs=pl.BlockSpec((atoms, 128), lambda i: (0, 0)),
        out_shape=jax.ShapeDtypeStruct((atoms, 128), F32),
        scratch_shapes=[
            pltpu.VMEM((2 * atoms, ROWS), F32),
            pltpu.VMEM((8, 8, CHUNK), F32),
        ],
        compiler_params=params(),
        name="boundary",
    )(place, atom_rows, gather, coef, slot_line, boundary_bessel.transpose(1, 0, 2), pot, index_line)
    parts = lax.all_to_all(partial_raw, "pencil", split_axis=0, concat_axis=0, tiled=True)
    boundary = jnp.sum(parts.reshape(count, own_atoms, 128), axis=0)[:, :LM].T

    steps = jnp.asarray(np.broadcast_to(np.arange(NG)[:, None], (NG, 128)).astype(BF16))
    along_z = jnp.asarray(along_z)
    if count == 16:
        flipped = lambda bit: [(i, i ^ bit) for i in range(count)]
        near = jnp.stack(
            [sent] + [lax.ppermute(sent, "pencil", flipped(bit)) for bit in (4, 8, 12)]
        )
        far = lax.ppermute(near, "pencil", flipped(2))
        begun = planes_call(count, place, near, 0, steps)
        own, other = planes_call(
            count, place, far, 2, steps, True, along_z, begun, partial_raw
        )
    else:
        groups = [list(range(c, count, 2)) for c in range(2)]
        recv = lax.all_gather(sent, "pencil", axis_index_groups=groups)
        own, other = planes_call(
            count, place, recv, None, steps, True, along_z, None, partial_raw
        )
    other = lax.ppermute(other, "pencil", [(i, i ^ 1) for i in range(count)])

    vmem = pl.BlockSpec(memory_space=pltpu.VMEM)
    anywhere = pl.BlockSpec(memory_space=pl.ANY)
    potential = pl.pallas_call(
        functools.partial(last_kernel, count),
        in_specs=[smem(), vmem, vmem, vmem, anywhere],
        out_specs=anywhere,
        out_shape=jax.ShapeDtypeStruct((NG * rows, NG), F32),
        scratch_shapes=[
            pltpu.VMEM((2, NG * rows, 128), F32),
            pltpu.VMEM((2, NG, NG), BF16),
            pltpu.SemaphoreType.DMA((2,)),
        ],
        compiler_params=params(),
        name="last",
    )(place, own, other, jnp.asarray(along_x), parts)
    return (potential.reshape(NG, rows, NG), boundary)


def solution(mesh):
    placed = (
        P(None, ("cells", "pencil")),
        P(None, ("cells", "pencil")),
        P(("cells", "pencil")),
        P("cells"),
        P(None, None, ("cells", "pencil")),
        P(None, None, ("cells", "pencil")),
        P(None, ("cells", "pencil")),
        P(("cells", "pencil")),
    )
    return jax.shard_map(
        body,
        mesh=mesh,
        in_specs=placed,
        out_specs=(P("cells", "pencil", None), P(None, ("cells", "pencil"))),
        check_vma=False,
    )
```

```python
import functools
import math

import jax
import jax.numpy as jnp
import numpy as np
from jax import lax
from jax.experimental import pallas as pl
from jax.experimental.pallas import tpu as pltpu
from jax.sharding import PartitionSpec as P

NG = 256
LMAX = 8
LM = 81
KINDS = 3
ROWS = 256
CHUNK = 2048
PITCH = NG // 2 + 8
HIGH = lax.Precision.HIGHEST
TWO_PI = 2.0 * math.pi
F32 = jnp.float32
BF16 = jnp.bfloat16
I32 = jnp.int32
VMEM_BYTES = 56 * 1024 * 1024


def norm(degree, m_order):
    base = (
        (2 * degree + 1)
        / (4 * math.pi)
        * math.factorial(degree - m_order)
        / math.factorial(degree + m_order)
    )
    return math.sqrt(base) * (math.sqrt(2.0) if m_order else 1.0)


def table_layout():
    tile_rows = [(d, 0) for d in range(1, 9)]
    tile_rows += [(8, m) for m in range(1, 9)] + [(8, -m) for m in range(1, 9)]
    tile_rows += [(4, r + 1) if r < 4 else (4, -(8 - r)) for r in range(8)]
    for low in (1, 2, 3):
        for sign in (1, -1):
            tile_rows += [
                (low, sign * (r + 1)) if r < low else (8 - low, sign * (8 - r)) for r in range(8)
            ]
    rows = {}
    for kind in range(KINDS):
        for at, (degree, m_order) in enumerate(tile_rows):
            rows[kind * 88 + at] = (kind, degree, m_order)
    rows[80] = (0, 0, 0)
    rows[168] = (1, 0, 0)
    rows[81] = (2, 0, 0)
    return rows


def placement_tables():
    spread = np.zeros((KINDS, 128, ROWS), np.float32)
    even = np.zeros((KINDS, ROWS, 128), np.float32)
    odd = np.zeros((KINDS, ROWS, 128), np.float32)
    for row, (kind, degree, m_order) in table_layout().items():
        lm = degree * degree + degree + m_order
        spread[kind, lm, row] = 1.0
        sign = -1.0 if degree % 4 in (1, 2) else 1.0
        (even if degree % 2 == 0 else odd)[kind, row, lm] = sign
    return spread, np.concatenate([even, odd], 0)


def recurrence_table():
    out = np.zeros((8, 128), np.float64)
    for direction in range(2):
        for r in range(8):
            m = r + 1 if direction == 0 else 8 - r
            start = float(np.prod(np.arange(1, 2 * m, 2)))
            for degree in range(1, 9):
                at = 3 * (8 * direction + degree - 1)
                if degree == m:
                    out[r, at + 2] = start * norm(m, m)
                elif degree > m:
                    out[r, at] = (
                        (2 * degree - 1) / (degree - m) * norm(degree, m) / norm(degree - 1, m)
                    )
                    if degree > m + 1:
                        out[r, at + 1] = (
                            (degree + m - 1) / (degree - m) * norm(degree, m) / norm(degree - 2, m)
                        )
    return out.astype(np.float32)


def fit_even(values, count):
    x = np.cos(np.pi * (np.arange(400) + 0.5) / 400) * 0.125 + 0.125
    basis = np.polynomial.chebyshev.Chebyshev.fit(x, values(np.sqrt(x)), count - 1, domain=[0, 0.25])
    return [float(c) for c in basis.convert(kind=np.polynomial.Polynomial, domain=[-1, 1]).coef]


SIN_FIT = fit_even(lambda x: np.sin(np.pi * x) / x, 5)
COS_FIT = fit_even(lambda x: np.cos(np.pi * x), 5)


def horner(coefficients, x):
    total = coefficients[-1]
    for coefficient in coefficients[-2::-1]:
        total = total * x + coefficient
    return total


def turn(t):
    t = t - jnp.floor(t + 0.5)
    square = t * t
    half_sin = t * horner(SIN_FIT, square)
    half_cos = horner(COS_FIT, square)
    return 1.0 - 2.0 * half_sin * half_sin, 2.0 * half_sin * half_cos


def split(x):
    high = x.astype(BF16)
    return high, (x - high.astype(F32)).astype(BF16)


def signed(index):
    return jnp.where(index >= NG // 2, index - NG, index).astype(F32)


def frequencies(position, owner, count):
    jx = (position >> 16) * count + owner
    jy = (position >> 8) & 255
    jz = position & 255
    return jx, signed(jx), signed(jy), signed(jz)


def table_of(freq, radial_ref, coef_ref, rows_scratch):
    freq_x, freq_y, freq_z = freq
    size_sq = freq_x * freq_x + freq_y * freq_y + freq_z * freq_z
    inv_size = 1.0 / jnp.sqrt(jnp.maximum(size_sq, 1.0))
    unit_x, unit_y, unit_z = freq_x * inv_size, freq_y * inv_size, freq_z * inv_size
    radius_sq = unit_x * unit_x + unit_y * unit_y + unit_z * unit_z
    width = unit_x.shape[1]
    cosine, sine = unit_x, unit_y
    for m in range(1, 9):
        rows_scratch[0, m - 1 : m, :] = cosine
        rows_scratch[1, m - 1 : m, :] = sine
        rows_scratch[2, 8 - m : 9 - m, :] = cosine
        rows_scratch[3, 8 - m : 9 - m, :] = sine
        cosine, sine = cosine * unit_x - sine * unit_y, sine * unit_x + cosine * unit_y
    before, current = jnp.zeros_like(unit_z), jnp.ones_like(unit_z)
    for degree in range(1, 9):
        before, current = (
            current,
            (2 * degree - 1) / degree * unit_z * current
            - (degree - 1) / degree * radius_sq * before,
        )
        rows_scratch[4, degree - 1 : degree, :] = norm(degree, 0) * current
    wide_z = jnp.broadcast_to(unit_z, (8, width))
    wide_sq = jnp.broadcast_to(radius_sq, (8, width))
    plain = []
    for direction in range(2):
        before = jnp.zeros((8, width), F32)
        current = jnp.zeros((8, width), F32)
        by_degree = [None]
        for degree in range(1, 9 - direction):
            at = 3 * (8 * direction + degree - 1)
            following = coef_ref[:, at + 2 : at + 3] + (coef_ref[:, at : at + 1] * wide_z) * current
            if degree > 2:
                following = following - (coef_ref[:, at + 1 : at + 2] * wide_sq) * before
            before, current = current, following
            by_degree.append(current)
        plain.append(by_degree)
    forward, reverse = plain
    cos_f, sin_f, cos_r, sin_r = (rows_scratch[i] for i in range(4))
    sub = lax.broadcasted_iota(I32, (8, width), 0)
    harm = [rows_scratch[4], forward[8] * cos_f, forward[8] * sin_f]
    harm.append(jnp.where(sub < 4, forward[4] * cos_f, reverse[4] * sin_r))
    for low in (1, 2, 3):
        harm.append(jnp.where(sub < low, forward[low] * cos_f, reverse[8 - low] * cos_r))
        harm.append(jnp.where(sub < low, forward[low] * sin_f, reverse[8 - low] * sin_r))
    zeros = jnp.zeros((8, width), F32)
    pieces = []
    first = norm(0, 0)
    for kind in range(KINDS):
        line = [
            jnp.broadcast_to(radial_ref[d, kind : kind + 1, :], (8, width)) for d in range(1, 9)
        ]
        line = [None] + line
        for d in range(1, 9):
            rows_scratch[5 + kind, d - 1 : d, :] = radial_ref[d, kind : kind + 1, :]
        pieces.append(harm[0] * rows_scratch[5 + kind])
        pieces.append(harm[1] * line[8])
        pieces.append(harm[2] * line[8])
        pieces.append(harm[3] * line[4])
        for low in (1, 2, 3):
            both = jnp.where(sub < low, line[low], line[8 - low])
            pieces.append(harm[2 + 2 * low] * both)
            pieces.append(harm[3 + 2 * low] * both)
        if kind < 2:
            own = jnp.broadcast_to(radial_ref[0, kind : kind + 1, :], (8, width)) * first
            extra = jnp.where(sub == 0, own, zeros)
            if kind == 0:
                third = jnp.broadcast_to(radial_ref[0, 2:3, :], (8, width)) * first
                extra = jnp.where(sub == 1, third, extra)
            pieces.append(extra)
    return split(jnp.concatenate(pieces, 0))


def angles(atoms_ref, freq):
    freq_x, freq_y, freq_z = freq
    return turn(
        atoms_ref[:, LM : LM + 1] * freq_x
        + atoms_ref[:, LM + 1 : LM + 2] * freq_y
        + atoms_ref[:, LM + 2 : LM + 3] * freq_z
    )


def gather_kernel(
    count, place_ref, moments_ref, positions_ref, species_ref, index_ref, out_ref, key_ref, held
):
    own = moments_ref.shape[0]
    lane = lax.broadcasted_iota(I32, (own, 128), 1)
    diagonal = lax.broadcasted_iota(I32, (own, own), 0) == lax.broadcasted_iota(I32, (own, own), 1)
    total = jnp.zeros((own, 128), F32)
    rows = [positions_ref[c : c + 1, :] for c in range(3)] + [species_ref[...].astype(F32)]
    for c, row in enumerate(rows):
        spread = jnp.where(diagonal, jnp.broadcast_to(row, (own, own)), 0.0)
        column = jnp.sum(spread, axis=1, keepdims=True)
        total = jnp.where(lane == LM + c, column, total)
    held[...] = total
    held[:, 0:LM] = moments_ref[...]
    out_ref[...] = jnp.broadcast_to(held[...][None], out_ref.shape)
    index = index_ref[...]
    jx = (index >> 16) * count + place_ref[0]
    jy = (index >> 8) & 255
    jz = index & 255
    folded = jnp.where(jx > NG // 2, ((-jy & 255) << 8) | (-jz & 255), (jy << 8) | jz)
    key_ref[...] = ((index >> 16) << 16) | folded


def charge_kernel(
    count,
    place_ref,
    atoms_ref,
    spread_ref,
    coef_ref,
    radial_ref,
    inter_ref,
    index_ref,
    key_ref,
    order_ref,
    pot_ref,
    sent_ref,
    weights,
    rows_scratch,
    values,
):
    step = pl.program_id(0)
    atoms = atoms_ref.shape[0]
    per_chunk = CHUNK // 128

    @pl.when(step == 0)
    def _():
        kind = atoms_ref[:, LM + 3 : LM + 4]
        total = jnp.zeros((atoms, ROWS), F32)
        for s in range(KINDS):
            moved = jnp.dot(
                atoms_ref[...], spread_ref[s], precision=HIGH, preferred_element_type=F32
            )
            total = total + jnp.where(kind == float(s), moved, 0.0)
        high, low = split(total)
        weights[0:atoms, :] = high
        weights[atoms : 2 * atoms, :] = low

    jx, *freq = frequencies(index_ref[...], place_ref[0], count)
    table_high, table_low = table_of(freq, radial_ref, coef_ref, rows_scratch)
    main = jnp.dot(weights[...], table_high, preferred_element_type=F32)
    rest = jnp.dot(weights[0:atoms, :], table_low, preferred_element_type=F32)
    shape_part = main[0:atoms] + (main[atoms:] + rest)
    cosine, sine = angles(atoms_ref, freq)
    pseudo_re = jnp.sum(shape_part * cosine, axis=0, keepdims=True)
    pseudo_im = -jnp.sum(shape_part * sine, axis=0, keepdims=True)
    freq_x, freq_y, freq_z = freq
    size_sq = freq_x * freq_x + freq_y * freq_y + freq_z * freq_z
    kernel = jnp.where(size_sq > 0, 1.0 / jnp.maximum(size_sq, 1.0), 0.0)
    pot_re = (inter_ref[0:1, :] + pseudo_re) * kernel
    pot_im = (inter_ref[1:2, :] + pseudo_im) * kernel
    pot_ref[0:1, :] = pot_re
    pot_ref[1:2, :] = pot_im
    folded_im = jnp.where(jx > NG // 2, -pot_im, pot_im)
    for j in range(per_chunk):
        line = pl.ds(step * per_chunk + j, 1)
        values[0, line, :] = pot_re[:, j * 128 : (j + 1) * 128]
        values[1, line, :] = folded_im[:, j * 128 : (j + 1) * 128]

    @pl.when(step == pl.num_programs(0) - 1)
    def _():
        order = order_ref[...]
        lines = order.shape[0]
        lane = order & 127
        line_of = order >> 7

        def one_line(r, carried):
            taken_re, taken_im = carried
            here = line_of == r
            row_re = jnp.broadcast_to(values[0, pl.ds(r, 1), :], (lines, 128))
            row_im = jnp.broadcast_to(values[1, pl.ds(r, 1), :], (lines, 128))
            taken_re = jnp.where(here, jnp.take_along_axis(row_re, lane, axis=1), taken_re)
            taken_im = jnp.where(here, jnp.take_along_axis(row_im, lane, axis=1), taken_im)
            return taken_re, taken_im

        empty = jnp.zeros((lines, 128), F32)
        taken_re, taken_im = lax.fori_loop(0, lines, one_line, (empty, empty), unroll=8)
        key = key_ref[...]
        sent_ref[0:lines, :] = taken_re
        sent_ref[lines : 2 * lines, :] = taken_im
        sent_ref[2 * lines : 3 * lines, :] = key.astype(F32)
        begins = (lax.broadcasted_iota(I32, (8, 128), 1) * 256).astype(F32)
        ends = begins + 255.0
        first = jnp.zeros((8, 128), F32)
        last = jnp.zeros((8, 128), F32)
        for k in range(1, NG // count):
            below = jnp.sum((key < (k << 16)).astype(F32), axis=(0, 1), keepdims=True)
            first = first + jnp.where(below <= begins, 1.0, 0.0)
            last = last + jnp.where(below <= ends, 1.0, 0.0)
        sub = lax.broadcasted_iota(I32, (8, 128), 0)
        sent_ref[3 * lines :, :] = jnp.where(sub == 0, first, last)


def boundary_kernel(
    count,
    place_ref,
    atoms_ref,
    gather_ref,
    coef_ref,
    slot_ref,
    bessel_ref,
    pot_ref,
    index_ref,
    out_ref,
    total,
    rows_scratch,
):
    step = pl.program_id(0)
    atoms = atoms_ref.shape[0]
    _, *freq = frequencies(index_ref[...], place_ref[0], count)
    table_high, table_low = table_of(freq, bessel_ref, coef_ref, rows_scratch)
    cosine, sine = angles(atoms_ref, freq)
    pot_re, pot_im = pot_ref[0:1, :], pot_ref[1:2, :]
    real_part = pot_re * cosine - pot_im * sine
    imag_part = pot_re * sine + pot_im * cosine
    high, low = split(jnp.concatenate([real_part, imag_part], 0))
    dims = (((1,), (1,)), ((), ()))
    both = lax.dot_general(
        jnp.concatenate([high, low], 0), table_high, dims, preferred_element_type=F32
    )
    rest = lax.dot_general(high, table_low, dims, preferred_element_type=F32)
    add = both[0 : 2 * atoms] + (both[2 * atoms :] + rest)

    @pl.when(step == 0)
    def _():
        total[...] = add

    @pl.when(step > 0)
    def _():
        total[...] += add

    @pl.when(step == pl.num_programs(0) - 1)
    def _():
        kind = atoms_ref[:, LM + 3 : LM + 4]
        raw = jnp.zeros((atoms, 128), F32)
        for s in range(KINDS):
            part = jnp.dot(
                total[0:atoms, :], gather_ref[s], precision=HIGH, preferred_element_type=F32
            ) + jnp.dot(
                total[atoms:, :], gather_ref[KINDS + s], precision=HIGH, preferred_element_type=F32
            )
            raw = raw + jnp.where(kind == float(s), part, 0.0)
        slots = lax.broadcasted_iota(I32, (atoms, atoms), 0)
        moved = (slots == slot_ref[...]).astype(F32)
        out_ref[...] = jnp.dot(moved, raw, precision=HIGH, preferred_element_type=F32)


def planes_kernel(count, pattern, finish, *refs):
    if finish:
        place_ref, start_ref, recv_ref, step_ref, wave_ref, before_ref, _ = refs[:7]
        own_ref, other_ref, box, front, back, fields, wave, earlier, sem = refs[7:]
    else:
        place_ref, start_ref, recv_ref, step_ref, box, front, back, fields = refs
    rows = NG // count
    chip_rows = 2 * rows
    sources = recv_ref.shape[0]
    lines = (recv_ref.shape[1] - 8) // 3
    half_planes = NG // 4
    tiles = lines // 2
    together = math.gcd(tiles, 16)
    place = place_ref[0]
    core = place % 2
    base = (place // 2) * chip_rows

    if finish and before_ref is not None:
        fetch = pltpu.make_async_copy(before_ref, earlier, sem)
        fetch.start()
    box[...] = jnp.zeros_like(box)

    sub = lax.broadcasted_iota(I32, (8, 128), 0)
    if chip_rows == 8:
        start_rows = (base + (sub + core * rows) % chip_rows).astype(F32) * (1.0 / NG)
    else:
        start_rows = (base + core * rows + sub).astype(F32) * (1.0 / NG)
    across = (1 - 2 * core).astype(F32) * (rows / NG)

    def all_fields(s, _):
        keys = recv_ref[s, 2 * lines : 3 * lines, :].astype(I32)
        jy = ((keys >> 8) & 255).astype(F32)
        fields[s, 0] = jy
        fields[s, 1] = (keys & 255).astype(F32)
        fields[s, 2] = (keys >> 16).astype(F32)
        if chip_rows > 8:
            fields[s, 3], fields[s, 4] = turn(jy * (8.0 / NG))
            fields[s, 5], fields[s, 6] = turn(jy * across)
        return 0

    lax.fori_loop(0, sources, all_fields, 0)

    def one_chunk(s, i, held):
        v_re = recv_ref[s, pl.ds(i, 1), :]
        v_im = recv_ref[s, pl.ds(lines + i, 1), :]
        jy, c_step, s_step, c_far, s_far = (
            fields[s, f, pl.ds(i, 1), :] if f == 0 or chip_rows > 8 else None
            for f in (0, 3, 4, 5, 6)
        )
        c, s = turn(jnp.broadcast_to(jy, (8, 128)) * start_rows)
        parts = [(v_re * c - v_im * s, v_re * s + v_im * c)]
        if chip_rows > 8:
            while 8 * len(parts) < rows:
                re, im = parts[-1]
                parts.append((re * c_step - im * s_step, re * s_step + im * c_step))
            parts += [(re * c_far - im * s_far, re * s_far + im * c_far) for re, im in parts]
        high, low = split(jnp.concatenate([re for re, _ in parts] + [im for _, im in parts], 0))
        held[i] = jnp.concatenate([high, low], 0)

    def edge(s, t, which):
        return start_ref[s, which, t].astype(I32)

    def plane_at(s, k):
        owner = place ^ (4 * s + pattern) if pattern is not None else 2 * s + core
        jx = k * count + owner
        return jnp.where(jx > NG // 2, NG - jx, jx) // 2

    def add_tile(s, t, wanted, held):
        left, right = [], []
        for i in (2 * t, 2 * t + 1):
            spot = jnp.broadcast_to(fields[s, 1, pl.ds(i, 1), :], (16, 128)).astype(BF16)
            hits = [
                jnp.where(
                    step_ref[16 * r : 16 * r + 16, :] == spot,
                    jnp.ones((16, 128), BF16),
                    jnp.zeros((16, 128), BF16),
                )
                for r in range(NG // 16)
            ]
            right.append(jnp.concatenate(hits, 0))
            plane = jnp.broadcast_to(fields[s, 2, pl.ds(i, 1), :], (16, 128))
            phased = held[i]
            masked = []
            for k, used in wanted:
                mask = jnp.where(plane == k.astype(F32), used, 0.0).astype(BF16)
                masked.append(phased * jnp.concatenate([mask] * (phased.shape[0] // 16), 0))
            left.append(jnp.concatenate(masked, 0))
        out = lax.dot_general(
            jnp.concatenate(left, 1),
            jnp.concatenate(right, 1),
            (((1,), (1,)), ((), ())),
            preferred_element_type=F32,
        )
        size = 2 * chip_rows
        for j, (k, _) in enumerate(wanted):
            box[plane_at(s, k)] += (
                out[2 * j * size : (2 * j + 1) * size] + out[(2 * j + 1) * size : (2 * j + 2) * size]
            )

    def one_source(s, held, following, filled):
        def some_tiles(g, most):
            for j in range(together):
                t = g * together + j
                first, last = edge(s, t, 0), edge(s, t, 1)
                second = jnp.where(last > first, 1.0, 0.0)
                add_tile(s, t, [(first, 1.0), (last, second)], held)
                one_chunk(following, 2 * t, filled)
                one_chunk(following, 2 * t + 1, filled)
                most = jnp.maximum(most, last - first)
            return most

        most = lax.fori_loop(0, tiles // together, some_tiles, jnp.int32(0))

        @pl.when(most > 1)
        def _():
            def one_tile(t, _):
                def between(k, _):
                    add_tile(s, t, [(k, 1.0)], held)
                    return 0

                return lax.fori_loop(edge(s, t, 0) + 1, edge(s, t, 1), between, 0)

            lax.fori_loop(0, tiles, one_tile, 0)

    def first_chunks(g, _):
        for j in range(8):
            one_chunk(0, 8 * g + j, front)
        return 0

    lax.fori_loop(0, lines // 8, first_chunks, 0)

    def two_sources(t, _):
        one_source(2 * t, front, 2 * t + 1, back)
        one_source(2 * t + 1, back, jnp.minimum(2 * t + 2, sources - 1), front)
        return 0

    lax.fori_loop(0, sources // 2, two_sources, 0)
    if not finish:
        return

    cos_z, sin_z = wave_ref[:, :NG], wave_ref[:, NG:]
    for j, table in enumerate((wave_ref[...], jnp.concatenate([-sin_z, cos_z], 1))):
        high, low = split(table)
        for k, part in enumerate((high, high, low)):
            wave[(3 * j + k) * NG : (3 * j + k + 1) * NG, :] = part
    if before_ref is not None:
        fetch.wait()

    def along_z(at, number):
        block = box[pl.ds(at, number)]
        if before_ref is not None:
            block = block + earlier[pl.ds(at, number)]
        left = []
        for part in (block[:, :chip_rows], block[:, chip_rows:]):
            high, low = split(part.reshape(number * chip_rows, NG))
            left += [high, low, high]
        out = jnp.dot(jnp.concatenate(left, 1), wave[...], preferred_element_type=F32)
        out = out.reshape(number, chip_rows, 2 * NG)
        return out[:, :, :NG], out[:, :, NG:]

    def keep(at, value):
        line = pl.ds(at, rows, stride=PITCH)
        for h in range(2):
            own_ref[h, line, :] = value[:rows, h * 128 : (h + 1) * 128]
            other_ref[h, line, :] = value[rows:, h * 128 : (h + 1) * 128]

    group = 16

    def some_planes(g, _):
        re, im = along_z(g * group, group)
        for j in range(group):
            keep(2 * (g * group + j), re[j])
            keep(2 * (g * group + j) + 1, im[j])
        return 0

    lax.fori_loop(0, half_planes // group, some_planes, 0, unroll=2)

    @pl.when(core == 0)
    def _():
        re, _ = along_z(half_planes, 1)
        keep(1, re[0])


def planes_call(count, place, recv, pattern, steps, finish=False, wave=None, before=None, after=None):
    rows = NG // count
    sources = recv.shape[0]
    lines = (recv.shape[1] - 8) // 3
    half_rows = rows * PITCH
    box = (NG // 4 + 1, 4 * rows, NG)
    vmem = pl.BlockSpec(memory_space=pltpu.VMEM)
    held = pltpu.VMEM((lines, 8 * rows, 128), BF16)
    scratch = [held, held, pltpu.VMEM((sources, 7, lines, 128), F32)]
    start_spec = pl.BlockSpec(
        (sources, 8, 128), lambda i: (0, 3 * lines // 8, 0), memory_space=pltpu.SMEM
    )
    recv_spec = pl.BlockSpec(recv.shape, lambda i: (0, 0, 0))
    step_spec = pl.BlockSpec(steps.shape, lambda i: (0, 0))
    in_specs = [smem(), start_spec, recv_spec, step_spec]
    operands = [place, recv, recv, steps]
    kernel = functools.partial(planes_kernel, count, pattern, finish)
    if not finish:
        return pl.pallas_call(
            kernel,
            grid=(1,),
            in_specs=in_specs,
            out_specs=pl.BlockSpec(box, lambda i: (0, 0, 0)),
            out_shape=jax.ShapeDtypeStruct(box, F32),
            scratch_shapes=scratch,
            compiler_params=params(),
            name="planes_near",
        cost_estimate=cost(15),
        )(*operands)
    scratch = [pltpu.VMEM(box, F32)] + scratch + [pltpu.VMEM((6 * NG, 2 * NG), BF16)]
    anywhere = pl.BlockSpec(memory_space=pl.ANY)
    in_specs.append(pl.BlockSpec(wave.shape, lambda i: (0, 0)))
    operands.append(wave)
    if before is None:
        inner = kernel
        at = len(in_specs)

        def kernel(*refs):
            inner(*refs[:at], None, *refs[at:], None, None)

    else:
        in_specs.append(anywhere)
        operands.append(before)
        scratch += [pltpu.VMEM(box, F32), pltpu.SemaphoreType.DMA]
    in_specs.append(anywhere)
    operands.append(after)
    return pl.pallas_call(
        kernel,
        grid=(1,),
        in_specs=in_specs,
        out_specs=[pl.BlockSpec((2, half_rows, 128), lambda i: (0, 0, 0))] * 2,
        out_shape=[jax.ShapeDtypeStruct((2, half_rows, 128), F32)] * 2,
        scratch_shapes=scratch,
        compiler_params=params(),
        name="planes",
        cost_estimate=cost(25),
    )(*operands)


def last_kernel(count, place_ref, own_ref, other_ref, wave_ref, _, out_ref, held, wave, sem):
    rows = NG // count
    wave[0], wave[1] = split(wave_ref[place_ref[0] % 2])

    def one_row(y, _):
        line = pl.ds(pl.multiple_of(y * PITCH, 8), NG // 2)
        mixed = [
            jnp.concatenate([own_ref[h, line, :], other_ref[h, line, :]], 0) for h in range(2)
        ]
        high, low = split(jnp.concatenate(mixed, 1))
        main = jnp.dot(wave[...].reshape(2 * NG, NG), high, preferred_element_type=F32)
        rest = jnp.dot(wave[0], low, preferred_element_type=F32)
        out = main[:NG] + (main[NG:] + rest)
        for h in range(2):
            held[h, pl.ds(y, NG, stride=rows), :] = out[:, h * 128 : (h + 1) * 128]
        return 0

    lax.fori_loop(0, rows, one_row, 0, unroll=4)
    copies = [
        pltpu.make_async_copy(held.at[h], out_ref.at[:, pl.ds(h * 128, 128)], sem.at[h])
        for h in range(2)
    ]
    for copy in copies:
        copy.start()
    for copy in copies:
        copy.wait()


def wave_tables():
    j = np.arange(NG)
    phase = 2 * np.pi / NG * ((j[:, None] * j[None, :]) % NG)
    along_z = np.concatenate([np.cos(phase), np.sin(phase)], 1)
    classes = []
    for core in range(2):
        table = np.zeros((NG, NG // 2))
        for i in range(NG // 4):
            phase_x = 2 * np.pi / NG * ((j * (2 * i + core)) % NG)
            table[:, 2 * i] = np.cos(phase_x)
            table[:, 2 * i + 1] = -np.sin(phase_x)
        if core == 0:
            table[:, 1] = np.cos(np.pi * j)
        classes.append(table)
    along_x = [np.concatenate([classes[c], classes[1 - c]], 1) for c in range(2)]
    return along_z.astype(np.float32), np.stack(along_x).astype(np.float32)


def smem():
    return pl.BlockSpec(memory_space=pltpu.SMEM)


def cost(micros):
    return pl.CostEstimate(flops=int(micros * 1e9), bytes_accessed=0, transcendentals=0)


def params():
    return pltpu.CompilerParams(vmem_limit_bytes=VMEM_BYTES)


def body(
    multipoles, positions, species, atom_slot, pseudo_radial, boundary_bessel, interstitial, g_index
):
    count = lax.axis_size("pencil")
    owner = lax.axis_index("pencil").astype(I32)
    place = owner.reshape(1)
    local_g = g_index.shape[0]
    lines = local_g // 128
    chunks = local_g // CHUNK
    atoms = atom_slot.shape[0]
    own_atoms = multipoles.shape[1]
    rows = NG // count
    spread, gather = placement_tables()
    coef = jnp.asarray(recurrence_table())
    along_z, along_x = wave_tables()

    vmem = pl.BlockSpec(memory_space=pltpu.VMEM)
    copies, key = pl.pallas_call(
        functools.partial(gather_kernel, count),
        in_specs=[smem(), vmem, vmem, vmem, vmem],
        out_specs=[vmem, vmem],
        out_shape=[
            jax.ShapeDtypeStruct((count, own_atoms, 128), F32),
            jax.ShapeDtypeStruct((lines, 128), I32),
        ],
        scratch_shapes=[pltpu.VMEM((own_atoms, 128), F32)],
        compiler_params=params(),
        name="atoms",
    )(
        place,
        multipoles.T,
        positions,
        species.reshape(1, own_atoms),
        g_index.reshape(lines, 128),
    )
    atom_rows = lax.all_to_all(copies, "pencil", split_axis=0, concat_axis=0, tiled=True)
    atom_rows = atom_rows.reshape(atoms, 128)

    key, order = lax.sort(
        (key.reshape(local_g), lax.iota(I32, local_g)), num_keys=1, is_stable=False
    )
    key = key.reshape(lines, 128)
    order = order.reshape(lines, 128)
    index_line = g_index.reshape(1, local_g)

    whole = lambda a: pl.BlockSpec(a.shape, lambda i: (0,) * a.ndim)
    line_spec = pl.BlockSpec((1, CHUNK), lambda i: (0, i))
    pair_spec = pl.BlockSpec((2, CHUNK), lambda i: (0, i))
    radial_spec = pl.BlockSpec((LMAX + 1, KINDS, CHUNK), lambda i: (0, 0, i))
    spread = jnp.asarray(spread)
    pot, sent = pl.pallas_call(
        functools.partial(charge_kernel, count),
        grid=(chunks,),
        in_specs=[
            smem(),
            whole(atom_rows),
            whole(spread),
            whole(coef),
            radial_spec,
            pair_spec,
            line_spec,
            whole(key),
            whole(order),
        ],
        out_specs=[pair_spec, pl.BlockSpec((3 * lines + 8, 128), lambda i: (0, 0))],
        out_shape=[
            jax.ShapeDtypeStruct((2, local_g), F32),
            jax.ShapeDtypeStruct((3 * lines + 8, 128), F32),
        ],
        scratch_shapes=[
            pltpu.VMEM((2 * atoms, ROWS), BF16),
            pltpu.VMEM((8, 8, CHUNK), F32),
            pltpu.VMEM((2, lines, 128), F32),
        ],
        compiler_params=params(),
        name="charge",
        cost_estimate=cost(10),
    )(place, atom_rows, spread, coef, pseudo_radial.transpose(1, 0, 2), interstitial, index_line, key, order)

    gather = jnp.asarray(gather)
    slot_line = atom_slot.reshape(1, atoms)
    partial_raw = pl.pallas_call(
        functools.partial(boundary_kernel, count),
        grid=(chunks,),
        in_specs=[
            smem(),
            whole(atom_rows),
            whole(gather),
            whole(coef),
            whole(slot_line),
            radial_spec,
            pair_spec,
            line_spec,
        ],
        out_specs=pl.BlockSpec((atoms, 128), lambda i: (0, 0)),
        out_shape=jax.ShapeDtypeStruct((atoms, 128), F32),
        scratch_shapes=[
            pltpu.VMEM((2 * atoms, ROWS), F32),
            pltpu.VMEM((8, 8, CHUNK), F32),
        ],
        compiler_params=params(),
        name="boundary",
        cost_estimate=cost(10),
    )(place, atom_rows, gather, coef, slot_line, boundary_bessel.transpose(1, 0, 2), pot, index_line)
    parts = lax.all_to_all(partial_raw, "pencil", split_axis=0, concat_axis=0, tiled=True)
    boundary = jnp.sum(parts.reshape(count, own_atoms, 128), axis=0)[:, :LM].T

    steps = jnp.asarray(np.broadcast_to(np.arange(NG)[:, None], (NG, 128)).astype(BF16))
    along_z = jnp.asarray(along_z)
    if count == 16:
        flipped = lambda bit: [(i, i ^ bit) for i in range(count)]
        pieces = [lax.ppermute(sent, "pencil", flipped(bit)) for bit in (4, 8, 12)]
        pieces, partial_raw = lax.optimization_barrier((pieces, partial_raw))
        near = jnp.stack([sent] + pieces)
        far = lax.ppermute(near, "pencil", flipped(2))
        begun = planes_call(count, place, near, 0, steps)
        own, other = planes_call(
            count, place, far, 2, steps, True, along_z, begun, parts
        )
    else:
        groups = [list(range(c, count, 2)) for c in range(2)]
        recv = lax.all_gather(sent, "pencil", axis_index_groups=groups)
        own, other = planes_call(
            count, place, recv, None, steps, True, along_z, None, partial_raw
        )
    other = lax.ppermute(other, "pencil", [(i, i ^ 1) for i in range(count)])

    vmem = pl.BlockSpec(memory_space=pltpu.VMEM)
    anywhere = pl.BlockSpec(memory_space=pl.ANY)
    potential = pl.pallas_call(
        functools.partial(last_kernel, count),
        in_specs=[smem(), vmem, vmem, vmem, anywhere],
        out_specs=anywhere,
        out_shape=jax.ShapeDtypeStruct((NG * rows, NG), F32),
        scratch_shapes=[
            pltpu.VMEM((2, NG * rows, 128), F32),
            pltpu.VMEM((2, NG, NG), BF16),
            pltpu.SemaphoreType.DMA((2,)),
        ],
        compiler_params=params(),
        name="last",
        cost_estimate=cost(7),
    )(place, own, other, jnp.asarray(along_x), parts)
    return (potential.reshape(NG, rows, NG), boundary)


def solution(mesh):
    placed = (
        P(None, ("cells", "pencil")),
        P(None, ("cells", "pencil")),
        P(("cells", "pencil")),
        P("cells"),
        P(None, None, ("cells", "pencil")),
        P(None, None, ("cells", "pencil")),
        P(None, ("cells", "pencil")),
        P(("cells", "pencil")),
    )
    return jax.shard_map(
        body,
        mesh=mesh,
        in_specs=placed,
        out_specs=(P("cells", "pencil", None), P(None, ("cells", "pencil"))),
        check_vma=False,
    )
```

```python
import functools
import math

import jax
import jax.numpy as jnp
import numpy as np
from jax import lax
from jax.experimental import pallas as pl
from jax.experimental.pallas import tpu as pltpu
from jax.sharding import PartitionSpec as P

NG = 256
LMAX = 8
LM = 81
KINDS = 3
ROWS = 256
CHUNK = 2048
HIGH = lax.Precision.HIGHEST
TWO_PI = 2.0 * math.pi
F32 = jnp.float32
BF16 = jnp.bfloat16
I32 = jnp.int32
PLANES_MB = 58
LAST_MB = 58


def norm(degree, m_order):
    base = (
        (2 * degree + 1)
        / (4 * math.pi)
        * math.factorial(degree - m_order)
        / math.factorial(degree + m_order)
    )
    return math.sqrt(base) * (math.sqrt(2.0) if m_order else 1.0)


def table_layout():
    tile_rows = [(d, 0) for d in range(1, 9)]
    tile_rows += [(8, m) for m in range(1, 9)] + [(8, -m) for m in range(1, 9)]
    tile_rows += [(4, r + 1) if r < 4 else (4, -(8 - r)) for r in range(8)]
    for low in (1, 2, 3):
        for sign in (1, -1):
            tile_rows += [
                (low, sign * (r + 1)) if r < low else (8 - low, sign * (8 - r)) for r in range(8)
            ]
    rows = {}
    for kind in range(KINDS):
        for at, (degree, m_order) in enumerate(tile_rows):
            rows[kind * 88 + at] = (kind, degree, m_order)
    rows[80] = (0, 0, 0)
    rows[168] = (1, 0, 0)
    rows[81] = (2, 0, 0)
    return rows


def placement_tables():
    spread = np.zeros((KINDS, 128, ROWS), np.float32)
    even = np.zeros((KINDS, ROWS, 128), np.float32)
    odd = np.zeros((KINDS, ROWS, 128), np.float32)
    for row, (kind, degree, m_order) in table_layout().items():
        lm = degree * degree + degree + m_order
        spread[kind, lm, row] = 1.0
        sign = -1.0 if degree % 4 in (1, 2) else 1.0
        (even if degree % 2 == 0 else odd)[kind, row, lm] = sign
    return spread, np.concatenate([even, odd], 0)


def recurrence_table():
    out = np.zeros((8, 128), np.float64)
    for direction in range(2):
        for r in range(8):
            m = r + 1 if direction == 0 else 8 - r
            start = float(np.prod(np.arange(1, 2 * m, 2)))
            for degree in range(1, 9):
                at = 3 * (8 * direction + degree - 1)
                if degree == m:
                    out[r, at + 2] = start * norm(m, m)
                elif degree > m:
                    out[r, at] = (
                        (2 * degree - 1) / (degree - m) * norm(degree, m) / norm(degree - 1, m)
                    )
                    if degree > m + 1:
                        out[r, at + 1] = (
                            (degree + m - 1) / (degree - m) * norm(degree, m) / norm(degree - 2, m)
                        )
    return out.astype(np.float32)


def fit_even(values, count):
    x = np.cos(np.pi * (np.arange(400) + 0.5) / 400) * 0.125 + 0.125
    basis = np.polynomial.chebyshev.Chebyshev.fit(x, values(np.sqrt(x)), count - 1, domain=[0, 0.25])
    return [float(c) for c in basis.convert(kind=np.polynomial.Polynomial, domain=[-1, 1]).coef]


SIN_FIT = fit_even(lambda x: np.sin(np.pi * x) / x, 5)
COS_FIT = fit_even(lambda x: np.cos(np.pi * x), 5)


def horner(coefficients, x):
    total = coefficients[-1]
    for coefficient in coefficients[-2::-1]:
        total = total * x + coefficient
    return total


def turn(t):
    t = t - jnp.floor(t + 0.5)
    square = t * t
    half_sin = t * horner(SIN_FIT, square)
    half_cos = horner(COS_FIT, square)
    return 1.0 - 2.0 * half_sin * half_sin, 2.0 * half_sin * half_cos


def split(x):
    high = x.astype(BF16)
    return high, (x - high.astype(F32)).astype(BF16)


def signed(index):
    return jnp.where(index >= NG // 2, index - NG, index).astype(F32)


def frequencies(position, owner, count):
    jx = (position >> 16) * count + owner
    jy = (position >> 8) & 255
    jz = position & 255
    return jx, signed(jx), signed(jy), signed(jz)


def table_of(freq, radial_ref, coef_ref, rows_scratch):
    freq_x, freq_y, freq_z = freq
    size_sq = freq_x * freq_x + freq_y * freq_y + freq_z * freq_z
    inv_size = 1.0 / jnp.sqrt(jnp.maximum(size_sq, 1.0))
    unit_x, unit_y, unit_z = freq_x * inv_size, freq_y * inv_size, freq_z * inv_size
    radius_sq = unit_x * unit_x + unit_y * unit_y + unit_z * unit_z
    width = unit_x.shape[1]
    cosine, sine = unit_x, unit_y
    for m in range(1, 9):
        rows_scratch[0, m - 1 : m, :] = cosine
        rows_scratch[1, m - 1 : m, :] = sine
        rows_scratch[2, 8 - m : 9 - m, :] = cosine
        rows_scratch[3, 8 - m : 9 - m, :] = sine
        cosine, sine = cosine * unit_x - sine * unit_y, sine * unit_x + cosine * unit_y
    before, current = jnp.zeros_like(unit_z), jnp.ones_like(unit_z)
    for degree in range(1, 9):
        before, current = (
            current,
            (2 * degree - 1) / degree * unit_z * current
            - (degree - 1) / degree * radius_sq * before,
        )
        rows_scratch[4, degree - 1 : degree, :] = norm(degree, 0) * current
    wide_z = jnp.broadcast_to(unit_z, (8, width))
    wide_sq = jnp.broadcast_to(radius_sq, (8, width))
    plain = []
    for direction in range(2):
        before = jnp.zeros((8, width), F32)
        current = jnp.zeros((8, width), F32)
        by_degree = [None]
        for degree in range(1, 9 - direction):
            at = 3 * (8 * direction + degree - 1)
            following = coef_ref[:, at + 2 : at + 3] + (coef_ref[:, at : at + 1] * wide_z) * current
            if degree > 2:
                following = following - (coef_ref[:, at + 1 : at + 2] * wide_sq) * before
            before, current = current, following
            by_degree.append(current)
        plain.append(by_degree)
    forward, reverse = plain
    cos_f, sin_f, cos_r, sin_r = (rows_scratch[i] for i in range(4))
    sub = lax.broadcasted_iota(I32, (8, width), 0)
    harm = [rows_scratch[4], forward[8] * cos_f, forward[8] * sin_f]
    harm.append(jnp.where(sub < 4, forward[4] * cos_f, reverse[4] * sin_r))
    for low in (1, 2, 3):
        harm.append(jnp.where(sub < low, forward[low] * cos_f, reverse[8 - low] * cos_r))
        harm.append(jnp.where(sub < low, forward[low] * sin_f, reverse[8 - low] * sin_r))
    zeros = jnp.zeros((8, width), F32)
    pieces = []
    first = norm(0, 0)
    for kind in range(KINDS):
        line = [
            jnp.broadcast_to(radial_ref[d, kind : kind + 1, :], (8, width)) for d in range(1, 9)
        ]
        line = [None] + line
        for d in range(1, 9):
            rows_scratch[5 + kind, d - 1 : d, :] = radial_ref[d, kind : kind + 1, :]
        pieces.append(harm[0] * rows_scratch[5 + kind])
        pieces.append(harm[1] * line[8])
        pieces.append(harm[2] * line[8])
        pieces.append(harm[3] * line[4])
        for low in (1, 2, 3):
            both = jnp.where(sub < low, line[low], line[8 - low])
            pieces.append(harm[2 + 2 * low] * both)
            pieces.append(harm[3 + 2 * low] * both)
        if kind < 2:
            own = jnp.broadcast_to(radial_ref[0, kind : kind + 1, :], (8, width)) * first
            extra = jnp.where(sub == 0, own, zeros)
            if kind == 0:
                third = jnp.broadcast_to(radial_ref[0, 2:3, :], (8, width)) * first
                extra = jnp.where(sub == 1, third, extra)
            pieces.append(extra)
    return split(jnp.concatenate(pieces, 0))


def angles(atoms_ref, freq):
    freq_x, freq_y, freq_z = freq
    return turn(
        atoms_ref[:, LM : LM + 1] * freq_x
        + atoms_ref[:, LM + 1 : LM + 2] * freq_y
        + atoms_ref[:, LM + 2 : LM + 3] * freq_z
    )


def gather_kernel(
    count, place_ref, moments_ref, positions_ref, species_ref, index_ref, out_ref, key_ref, held
):
    own = moments_ref.shape[0]
    lane = lax.broadcasted_iota(I32, (own, 128), 1)
    diagonal = lax.broadcasted_iota(I32, (own, own), 0) == lax.broadcasted_iota(I32, (own, own), 1)
    total = jnp.zeros((own, 128), F32)
    rows = [positions_ref[c : c + 1, :] for c in range(3)] + [species_ref[...].astype(F32)]
    for c, row in enumerate(rows):
        spread = jnp.where(diagonal, jnp.broadcast_to(row, (own, own)), 0.0)
        column = jnp.sum(spread, axis=1, keepdims=True)
        total = jnp.where(lane == LM + c, column, total)
    held[...] = total
    held[:, 0:LM] = moments_ref[...]
    out_ref[...] = jnp.broadcast_to(held[...][None], out_ref.shape)
    index = index_ref[...]
    jx = (index >> 16) * count + place_ref[0]
    jy = (index >> 8) & 255
    jz = index & 255
    folded = jnp.where(jx > NG // 2, ((-jy & 255) << 8) | (-jz & 255), (jy << 8) | jz)
    key_ref[...] = ((index >> 16) << 16) | folded


def charge_kernel(
    count,
    place_ref,
    atoms_ref,
    spread_ref,
    coef_ref,
    radial_ref,
    inter_ref,
    index_ref,
    key_ref,
    order_ref,
    pot_ref,
    sent_ref,
    cos_ref,
    sin_ref,
    weights,
    rows_scratch,
    values,
):
    step = pl.program_id(0)
    atoms = atoms_ref.shape[0]
    per_chunk = CHUNK // 128

    @pl.when(step == 0)
    def _():
        kind = atoms_ref[:, LM + 3 : LM + 4]
        total = jnp.zeros((atoms, ROWS), F32)
        for s in range(KINDS):
            moved = jnp.dot(
                atoms_ref[...], spread_ref[s], precision=HIGH, preferred_element_type=F32
            )
            total = total + jnp.where(kind == float(s), moved, 0.0)
        high, low = split(total)
        weights[0:atoms, :] = high
        weights[atoms : 2 * atoms, :] = low

    jx, *freq = frequencies(index_ref[...], place_ref[0], count)
    table_high, table_low = table_of(freq, radial_ref, coef_ref, rows_scratch)
    main = jnp.dot(weights[...], table_high, preferred_element_type=F32)
    rest = jnp.dot(weights[0:atoms, :], table_low, preferred_element_type=F32)
    shape_part = main[0:atoms] + (main[atoms:] + rest)
    cosine, sine = angles(atoms_ref, freq)
    cos_ref[...] = cosine
    sin_ref[...] = sine
    pseudo_re = jnp.sum(shape_part * cosine, axis=0, keepdims=True)
    pseudo_im = -jnp.sum(shape_part * sine, axis=0, keepdims=True)
    freq_x, freq_y, freq_z = freq
    size_sq = freq_x * freq_x + freq_y * freq_y + freq_z * freq_z
    kernel = jnp.where(size_sq > 0, 1.0 / jnp.maximum(size_sq, 1.0), 0.0)
    pot_re = (inter_ref[0:1, :] + pseudo_re) * kernel
    pot_im = (inter_ref[1:2, :] + pseudo_im) * kernel
    pot_ref[0:1, :] = pot_re
    pot_ref[1:2, :] = pot_im
    folded_im = jnp.where(jx > NG // 2, -pot_im, pot_im)
    for j in range(per_chunk):
        line = pl.ds(step * per_chunk + j, 1)
        values[0, line, :] = pot_re[:, j * 128 : (j + 1) * 128]
        values[1, line, :] = folded_im[:, j * 128 : (j + 1) * 128]

    @pl.when(step == pl.num_programs(0) - 1)
    def _():
        order = order_ref[...]
        lines = order.shape[0]
        lane = order & 127
        line_of = order >> 7

        def one_line(r, carried):
            taken_re, taken_im = carried
            here = line_of == r
            row_re = jnp.broadcast_to(values[0, pl.ds(r, 1), :], (lines, 128))
            row_im = jnp.broadcast_to(values[1, pl.ds(r, 1), :], (lines, 128))
            taken_re = jnp.where(here, jnp.take_along_axis(row_re, lane, 1, mode="promise_in_bounds"), taken_re)
            taken_im = jnp.where(here, jnp.take_along_axis(row_im, lane, 1, mode="promise_in_bounds"), taken_im)
            return taken_re, taken_im

        empty = jnp.zeros((lines, 128), F32)
        taken_re, taken_im = lax.fori_loop(0, lines, one_line, (empty, empty), unroll=8)
        key = key_ref[...]
        sent_ref[0:lines, :] = taken_re
        sent_ref[lines : 2 * lines, :] = taken_im
        sent_ref[2 * lines : 3 * lines, :] = key.astype(F32)
        begins = (lax.broadcasted_iota(I32, (8, 128), 1) * 256).astype(F32)
        ends = begins + 255.0
        first = jnp.zeros((8, 128), F32)
        last = jnp.zeros((8, 128), F32)
        for k in range(1, NG // count):
            below = jnp.sum((key < (k << 16)).astype(F32), axis=(0, 1), keepdims=True)
            first = first + jnp.where(below <= begins, 1.0, 0.0)
            last = last + jnp.where(below <= ends, 1.0, 0.0)
        sub = lax.broadcasted_iota(I32, (8, 128), 0)
        sent_ref[3 * lines :, :] = jnp.where(sub == 0, first, last)


def boundary_kernel(
    count,
    place_ref,
    atoms_ref,
    gather_ref,
    coef_ref,
    slot_ref,
    bessel_ref,
    pot_ref,
    index_ref,
    cos_ref,
    sin_ref,
    out_ref,
    total,
    rows_scratch,
):
    step = pl.program_id(0)
    atoms = atoms_ref.shape[0]
    _, *freq = frequencies(index_ref[...], place_ref[0], count)
    table_high, table_low = table_of(freq, bessel_ref, coef_ref, rows_scratch)
    cosine, sine = cos_ref[...], sin_ref[...]
    pot_re, pot_im = pot_ref[0:1, :], pot_ref[1:2, :]
    real_part = pot_re * cosine - pot_im * sine
    imag_part = pot_re * sine + pot_im * cosine
    high, low = split(jnp.concatenate([real_part, imag_part], 0))
    dims = (((1,), (1,)), ((), ()))
    both = lax.dot_general(
        jnp.concatenate([high, low], 0), table_high, dims, preferred_element_type=F32
    )
    rest = lax.dot_general(high, table_low, dims, preferred_element_type=F32)
    add = both[0 : 2 * atoms] + (both[2 * atoms :] + rest)

    @pl.when(step == 0)
    def _():
        total[...] = add

    @pl.when(step > 0)
    def _():
        total[...] += add

    @pl.when(step == pl.num_programs(0) - 1)
    def _():
        kind = atoms_ref[:, LM + 3 : LM + 4]
        raw = jnp.zeros((atoms, 128), F32)
        for s in range(KINDS):
            part = jnp.dot(
                total[0:atoms, :], gather_ref[s], precision=HIGH, preferred_element_type=F32
            ) + jnp.dot(
                total[atoms:, :], gather_ref[KINDS + s], precision=HIGH, preferred_element_type=F32
            )
            raw = raw + jnp.where(kind == float(s), part, 0.0)
        slots = lax.broadcasted_iota(I32, (atoms, atoms), 0)
        moved = (slots == slot_ref[...]).astype(F32)
        out_ref[...] = jnp.dot(moved, raw, precision=HIGH, preferred_element_type=F32)


def plane_type(place):
    return ((place >> 1) ^ ((place & 1) * (place >> 2))) & 1


def planes_kernel(count, pattern, *refs):
    place_ref, recv_ref, step_ref, wave_in, _, own_out, other_out = refs[:7]
    wave_ref, own_ref, other_ref, wave, start_ref, sem, box, front, back, fields = refs[7:]
    rows = NG // count
    chip_rows = 2 * rows
    sources = recv_ref.shape[0]
    lines = (recv_ref.shape[1] - 8) // 3
    halves = 1 if pattern is None else 2
    local_planes = NG // 4 // halves
    pitch = 2 * local_planes + 8
    tiles = lines // 2
    together = math.gcd(tiles, 16)
    place = place_ref[0]
    core = place % 2
    base = (place // 2) * chip_rows

    fetch = pltpu.make_async_copy(recv_ref.at[:, pl.ds(3 * lines, 8), :], start_ref, sem.at[0])
    fetch.start()
    fetch_wave = pltpu.make_async_copy(wave_in, wave_ref, sem.at[1])
    fetch_wave.start()
    box[...] = jnp.zeros_like(box)

    sub = lax.broadcasted_iota(I32, (8, 128), 0)
    if chip_rows == 8:
        start_rows = (base + (sub + core * rows) % chip_rows).astype(F32) * (1.0 / NG)
    else:
        start_rows = (base + core * rows + sub).astype(F32) * (1.0 / NG)
    across = (1 - 2 * core).astype(F32) * (rows / NG)

    def all_fields(s, _):
        keys = recv_ref[s, 2 * lines : 3 * lines, :].astype(I32)
        jy = ((keys >> 8) & 255).astype(F32)
        fields[s, 0] = jy
        fields[s, 1] = (keys & 255).astype(F32)
        fields[s, 2] = (keys >> 16).astype(F32)
        if chip_rows > 8:
            fields[s, 3], fields[s, 4] = turn(jy * (8.0 / NG))
            fields[s, 5], fields[s, 6] = turn(jy * across)
        return 0

    lax.fori_loop(0, sources, all_fields, 0)

    def one_chunk(s, i, held):
        v_re = recv_ref[s, pl.ds(i, 1), :]
        v_im = recv_ref[s, pl.ds(lines + i, 1), :]
        jy, c_step, s_step, c_far, s_far = (
            fields[s, f, pl.ds(i, 1), :] if f == 0 or chip_rows > 8 else None
            for f in (0, 3, 4, 5, 6)
        )
        c, s = turn(jnp.broadcast_to(jy, (8, 128)) * start_rows)
        parts = [(v_re * c - v_im * s, v_re * s + v_im * c)]
        if chip_rows > 8:
            while 8 * len(parts) < rows:
                re, im = parts[-1]
                parts.append((re * c_step - im * s_step, re * s_step + im * c_step))
            parts += [(re * c_far - im * s_far, re * s_far + im * c_far) for re, im in parts]
        high, low = split(jnp.concatenate([re for re, _ in parts] + [im for _, im in parts], 0))
        held[i] = jnp.concatenate([high, low], 0)

    def edge(s, t, which):
        return start_ref[s, which, t].astype(I32)

    def plane_at(s, k):
        if pattern is None:
            owner = 2 * s + core
        else:
            owner = place ^ pattern ^ (8 * (s >> 1) + (4 + 2 * core) * (s & 1))
        jx = k * count + owner
        return jnp.where(jx > NG // 2, NG - jx, jx) // (2 * halves)

    def add_tile(s, t, wanted, held):
        left, right = [], []
        for i in (2 * t, 2 * t + 1):
            spot = jnp.broadcast_to(fields[s, 1, pl.ds(i, 1), :], (16, 128)).astype(BF16)
            hits = [
                jnp.where(
                    step_ref[16 * r : 16 * r + 16, :] == spot,
                    jnp.ones((16, 128), BF16),
                    jnp.zeros((16, 128), BF16),
                )
                for r in range(NG // 16)
            ]
            right.append(jnp.concatenate(hits, 0))
            plane = jnp.broadcast_to(fields[s, 2, pl.ds(i, 1), :], (16, 128))
            phased = held[i]
            masked = []
            for k, used in wanted:
                mask = jnp.where(plane == k.astype(F32), used, 0.0).astype(BF16)
                masked.append(phased * jnp.concatenate([mask] * (phased.shape[0] // 16), 0))
            left.append(jnp.concatenate(masked, 0))
        out = lax.dot_general(
            jnp.concatenate(left, 1),
            jnp.concatenate(right, 1),
            (((1,), (1,)), ((), ())),
            preferred_element_type=F32,
        )
        size = 2 * chip_rows
        for j, (k, _) in enumerate(wanted):
            box[plane_at(s, k)] += (
                out[2 * j * size : (2 * j + 1) * size] + out[(2 * j + 1) * size : (2 * j + 2) * size]
            )

    def one_source(s, held, following, filled):
        def some_tiles(g, most):
            for j in range(together):
                t = g * together + j
                first, last = edge(s, t, 0), edge(s, t, 1)
                second = jnp.where(last > first, 1.0, 0.0)
                add_tile(s, t, [(first, 1.0), (last, second)], held)
                if filled is not None:
                    one_chunk(following, 2 * t, filled)
                    one_chunk(following, 2 * t + 1, filled)
                most = jnp.maximum(most, last - first)
            return most

        most = lax.fori_loop(0, tiles // together, some_tiles, jnp.int32(0))

        @pl.when(most > 1)
        def _():
            def one_tile(t, _):
                def between(k, _):
                    add_tile(s, t, [(k, 1.0)], held)
                    return 0

                return lax.fori_loop(edge(s, t, 0) + 1, edge(s, t, 1), between, 0)

            lax.fori_loop(0, tiles, one_tile, 0)

    def first_chunks(g, _):
        for j in range(8):
            one_chunk(0, 8 * g + j, front)
        return 0

    lax.fori_loop(0, lines // 8, first_chunks, 0)
    fetch.wait()

    def two_sources(t, _):
        one_source(2 * t, front, 2 * t + 1, back)
        one_source(2 * t + 1, back, 2 * t + 2, front)
        return 0

    lax.fori_loop(0, sources // 2 - 1, two_sources, 0)
    one_source(sources - 2, front, sources - 1, back)
    one_source(sources - 1, back, None, None)
    fetch_wave.wait()
    cos_z, sin_z = wave_ref[:, :NG], wave_ref[:, NG:]
    for j, table in enumerate((wave_ref[...], jnp.concatenate([-sin_z, cos_z], 1))):
        high, low = split(table)
        for k, part in enumerate((high, high, low)):
            wave[(3 * j + k) * NG : (3 * j + k + 1) * NG, :] = part

    def along_z(at, number):
        block = box[pl.ds(at, number)]
        left = []
        for part in (block[:, :chip_rows], block[:, chip_rows:]):
            high, low = split(part.reshape(number * chip_rows, NG))
            left += [high, low, high]
        out = jnp.dot(jnp.concatenate(left, 1), wave[...], preferred_element_type=F32)
        out = out.reshape(number, chip_rows, 2 * NG)
        return out[:, :, :NG], out[:, :, NG:]

    def keep(at, value):
        line = pl.ds(at, rows, stride=pitch)
        for h in range(2):
            own_ref[h, line, :] = value[:rows, h * 128 : (h + 1) * 128]
            other_ref[h, line, :] = value[rows:, h * 128 : (h + 1) * 128]

    group = 16

    def some_planes(g, _):
        re, im = along_z(g * group, group)
        for j in range(group):
            keep(2 * (g * group + j), re[j])
            keep(2 * (g * group + j) + 1, im[j])
        return 0

    lax.fori_loop(0, local_planes // group, some_planes, 0, unroll=2)
    has_middle = core == 0
    if pattern is not None:
        has_middle = has_middle & (plane_type(place) == (1 if pattern else 0))

    @pl.when(has_middle)
    def _():
        re, _ = along_z(local_planes, 1)
        keep(1, re[0])

    stores = [
        pltpu.make_async_copy(other_ref, other_out, sem.at[0]),
        pltpu.make_async_copy(own_ref, own_out, sem.at[1]),
    ]
    for store in stores:
        store.start()
    for store in stores:
        store.wait()


def planes_call(count, place, recv, pattern, steps, wave, after):
    rows = NG // count
    sources = recv.shape[0]
    lines = (recv.shape[1] - 8) // 3
    local_planes = NG // 4 // (1 if pattern is None else 2)
    half = jax.ShapeDtypeStruct((2, rows * (2 * local_planes + 8), 128), F32)
    vmem = pl.BlockSpec(memory_space=pltpu.VMEM)
    anywhere = pl.BlockSpec(memory_space=pl.ANY)
    held = pltpu.VMEM((lines, 8 * rows, 128), BF16)
    return pl.pallas_call(
        functools.partial(planes_kernel, count, pattern),
        in_specs=[smem(), vmem, vmem, anywhere, anywhere],
        out_specs=[anywhere, anywhere],
        out_shape=[half, half],
        scratch_shapes=[
            pltpu.VMEM((NG, 2 * NG), F32),
            pltpu.VMEM(half.shape, F32),
            pltpu.VMEM(half.shape, F32),
            pltpu.VMEM((6 * NG, 2 * NG), BF16),
            pltpu.SMEM((sources, 8, 128), F32),
            pltpu.SemaphoreType.DMA((2,)),
            pltpu.VMEM((local_planes + 1, 4 * rows, NG), F32),
            held,
            held,
            pltpu.VMEM((sources, 7, lines, 128), F32),
        ],
        compiler_params=params(PLANES_MB),
        name="planes_far" if pattern else "planes_near",
        cost_estimate=cost(15),
    )(place, recv, steps, wave, after)


def last_kernel(count, place_ref, wave_ref, *refs):
    halves = (len(refs) - 6) // 2
    given = refs[: 2 * halves]
    out_ref, held, wave, tables_ref, parts, sem = refs[2 * halves :]
    rows = NG // count
    size = NG // 2 // halves
    pitch = size + 8
    place = place_ref[0]
    group = 4
    fetch_tables = pltpu.make_async_copy(wave_ref, tables_ref, sem.at[0, 2 * halves])
    fetch_tables.start()
    fetches = []
    for g in range(rows // group):
        line = pl.ds(g * group * pitch, group * pitch)
        fetches.append(
            [
                pltpu.make_async_copy(part.at[:, line, :], parts.at[i, :, line, :], sem.at[g, i])
                for i, part in enumerate(given)
            ]
        )
        for fetch in fetches[-1]:
            fetch.start()
    fetch_tables.wait()
    tables = []
    for device in (place, place ^ 1):
        for half in range(halves):
            which = device & 1
            if halves == 2:
                which = 2 * which + (plane_type(device) ^ half)
            tables.append(tables_ref[which])
    wave[0], wave[1] = split(jnp.concatenate(tables, 0).T)

    def one_row(y):
        line = pl.ds(y * pitch, size)
        mixed = [
            jnp.concatenate([parts[i, h, line, :] for i in range(2 * halves)], 0) for h in range(2)
        ]
        high, low = split(jnp.concatenate(mixed, 1))
        main = jnp.dot(wave[...].reshape(2 * NG, NG), high, preferred_element_type=F32)
        rest = jnp.dot(wave[0], low, preferred_element_type=F32)
        out = main[:NG] + (main[NG:] + rest)
        for h in range(2):
            held[h, pl.ds(y, NG, stride=rows), :] = out[:, h * 128 : (h + 1) * 128]

    for g in range(rows // group):
        for fetch in fetches[g]:
            fetch.wait()
        for y in range(g * group, (g + 1) * group):
            one_row(y)
    copies = [
        pltpu.make_async_copy(held.at[h], out_ref.at[:, pl.ds(h * 128, 128)], sem.at[0, h])
        for h in range(2)
    ]
    for copy in copies:
        copy.start()
    for copy in copies:
        copy.wait()


def wave_tables(halves):
    j = np.arange(NG)
    phase = 2 * np.pi / NG * ((j[:, None] * j[None, :]) % NG)
    along_z = np.concatenate([np.cos(phase), np.sin(phase)], 1)
    along_x = []
    for core in range(2):
        for kind in range(halves):
            planes = np.arange(core, NG // 2, 2)
            if halves == 2 and core == 0:
                planes = planes[planes % 4 == 2 * kind]
            elif halves == 2:
                planes = planes[np.isin(planes % 8, (3, 5) if kind else (1, 7))]
            phase = 2 * np.pi / NG * ((planes[:, None] * j[None, :]) % NG)
            table = np.stack([np.cos(phase), -np.sin(phase)], 1).reshape(-1, NG)
            if planes[0] == 0:
                table[1] = np.cos(np.pi * j)
            along_x.append(table)
    return along_z.astype(np.float32), np.stack(along_x).astype(np.float32)


def smem():
    return pl.BlockSpec(memory_space=pltpu.SMEM)


def cost(micros):
    return pl.CostEstimate(flops=int(micros * 1e9), bytes_accessed=0, transcendentals=0)


def params(megabytes=56):
    return pltpu.CompilerParams(vmem_limit_bytes=megabytes * 1024 * 1024)


def body(
    multipoles, positions, species, atom_slot, pseudo_radial, boundary_bessel, interstitial, g_index
):
    count = lax.axis_size("pencil")
    owner = lax.axis_index("pencil").astype(I32)
    place = owner.reshape(1)
    local_g = g_index.shape[0]
    lines = local_g // 128
    chunks = local_g // CHUNK
    atoms = atom_slot.shape[0]
    own_atoms = multipoles.shape[1]
    rows = NG // count
    spread, gather = placement_tables()
    coef = jnp.asarray(recurrence_table())
    along_z, along_x = wave_tables(2 if count == 16 else 1)

    vmem = pl.BlockSpec(memory_space=pltpu.VMEM)
    copies, key = pl.pallas_call(
        functools.partial(gather_kernel, count),
        in_specs=[smem(), vmem, vmem, vmem, vmem],
        out_specs=[vmem, vmem],
        out_shape=[
            jax.ShapeDtypeStruct((count, own_atoms, 128), F32),
            jax.ShapeDtypeStruct((lines, 128), I32),
        ],
        scratch_shapes=[pltpu.VMEM((own_atoms, 128), F32)],
        compiler_params=params(),
        name="atoms",
    )(
        place,
        multipoles.T,
        positions,
        species.reshape(1, own_atoms),
        g_index.reshape(lines, 128),
    )
    atom_rows = lax.all_to_all(copies, "pencil", split_axis=0, concat_axis=0, tiled=True)
    atom_rows = atom_rows.reshape(atoms, 128)

    key, order = lax.sort(
        (key.reshape(local_g), lax.iota(I32, local_g)), num_keys=1, is_stable=False
    )
    key = key.reshape(lines, 128)
    order = order.reshape(lines, 128)
    index_line = g_index.reshape(1, local_g)

    whole = lambda a: pl.BlockSpec(a.shape, lambda i: (0,) * a.ndim)
    line_spec = pl.BlockSpec((1, CHUNK), lambda i: (0, i))
    pair_spec = pl.BlockSpec((2, CHUNK), lambda i: (0, i))
    radial_spec = pl.BlockSpec((LMAX + 1, KINDS, CHUNK), lambda i: (0, 0, i))
    spread = jnp.asarray(spread)
    atom_spec = pl.BlockSpec((atoms, CHUNK), lambda i: (0, i))
    pot, sent, cosine, sine = pl.pallas_call(
        functools.partial(charge_kernel, count),
        grid=(chunks,),
        in_specs=[
            smem(),
            whole(atom_rows),
            whole(spread),
            whole(coef),
            radial_spec,
            pair_spec,
            line_spec,
            whole(key),
            whole(order),
        ],
        out_specs=[
            pair_spec,
            pl.BlockSpec((3 * lines + 8, 128), lambda i: (0, 0)),
            atom_spec,
            atom_spec,
        ],
        out_shape=[
            jax.ShapeDtypeStruct((2, local_g), F32),
            jax.ShapeDtypeStruct((3 * lines + 8, 128), F32),
            jax.ShapeDtypeStruct((atoms, local_g), F32),
            jax.ShapeDtypeStruct((atoms, local_g), F32),
        ],
        scratch_shapes=[
            pltpu.VMEM((2 * atoms, ROWS), BF16),
            pltpu.VMEM((8, 8, CHUNK), F32),
            pltpu.VMEM((2, lines, 128), F32),
        ],
        compiler_params=params(),
        name="charge",
        cost_estimate=cost(10),
    )(place, atom_rows, spread, coef, pseudo_radial.transpose(1, 0, 2), interstitial, index_line, key, order)

    gather = jnp.asarray(gather)
    slot_line = atom_slot.reshape(1, atoms)
    partial_raw = pl.pallas_call(
        functools.partial(boundary_kernel, count),
        grid=(chunks,),
        in_specs=[
            smem(),
            whole(atom_rows),
            whole(gather),
            whole(coef),
            whole(slot_line),
            radial_spec,
            pair_spec,
            line_spec,
            atom_spec,
            atom_spec,
        ],
        out_specs=pl.BlockSpec((atoms, 128), lambda i: (0, 0)),
        out_shape=jax.ShapeDtypeStruct((atoms, 128), F32),
        scratch_shapes=[
            pltpu.VMEM((2 * atoms, ROWS), F32),
            pltpu.VMEM((8, 8, CHUNK), F32),
        ],
        compiler_params=params(),
        name="boundary",
        cost_estimate=cost(10),
    )(place, atom_rows, gather, coef, slot_line, boundary_bessel.transpose(1, 0, 2), pot, index_line, cosine, sine)
    parts = lax.all_to_all(partial_raw, "pencil", split_axis=0, concat_axis=0, tiled=True)
    boundary = jnp.sum(parts.reshape(count, own_atoms, 128), axis=0)[:, :LM].T

    steps = jnp.asarray(np.broadcast_to(np.arange(NG)[:, None], (NG, 128)).astype(BF16))
    along_z = jnp.asarray(along_z)
    sibling = [(i, i ^ 1) for i in range(count)]
    if count == 16:
        masks = [lambda i: 4 + 2 * (i & 1), lambda i: 8, lambda i: 12 + 2 * (i & 1)]
        pieces = [
            lax.ppermute(sent, "pencil", [(i, i ^ mask(i)) for i in range(count)])
            for mask in masks
        ]
        pieces, partial_raw = lax.optimization_barrier((pieces, partial_raw))
        near = jnp.stack([sent] + pieces)
        far = lax.ppermute(near, "pencil", [(i, i ^ 2) for i in range(count)])
        own_near, other_near = planes_call(count, place, near, 0, steps, along_z, partial_raw)
        other_near = lax.ppermute(other_near, "pencil", sibling)
        own_far, other_far = planes_call(count, place, far, 2, steps, along_z, parts)
        other_far = lax.ppermute(other_far, "pencil", sibling)
        waves = [own_near, own_far, other_near, other_far]
    else:
        groups = [list(range(c, count, 2)) for c in range(2)]
        recv = lax.all_gather(sent, "pencil", axis_index_groups=groups)
        own, other = planes_call(count, place, recv, None, steps, along_z, partial_raw)
        waves = [own, lax.ppermute(other, "pencil", sibling)]

    along_x = jnp.asarray(along_x)
    anywhere = pl.BlockSpec(memory_space=pl.ANY)
    potential = pl.pallas_call(
        functools.partial(last_kernel, count),
        in_specs=[smem()] + [anywhere] * (1 + len(waves)),
        out_specs=anywhere,
        out_shape=jax.ShapeDtypeStruct((NG * rows, NG), F32),
        scratch_shapes=[
            pltpu.VMEM((2, NG * rows, 128), F32),
            pltpu.VMEM((2, NG, NG), BF16),
            pltpu.VMEM(along_x.shape, F32),
            pltpu.VMEM((len(waves),) + waves[0].shape, F32),
            pltpu.SemaphoreType.DMA((rows // 4, len(waves) + 1)),
        ],
        compiler_params=params(LAST_MB),
        name="last",
        cost_estimate=cost(7),
    )(place, along_x, *waves)
    return (potential.reshape(NG, rows, NG), boundary)


def solution(mesh):
    placed = (
        P(None, ("cells", "pencil")),
        P(None, ("cells", "pencil")),
        P(("cells", "pencil")),
        P("cells"),
        P(None, None, ("cells", "pencil")),
        P(None, None, ("cells", "pencil")),
        P(None, ("cells", "pencil")),
        P(("cells", "pencil")),
    )
    return jax.shard_map(
        body,
        mesh=mesh,
        in_specs=placed,
        out_specs=(P("cells", "pencil", None), P(None, ("cells", "pencil"))),
        check_vma=False,
    )
```

```python
import functools
import math

import jax
import jax.numpy as jnp
import numpy as np
from jax import lax
from jax.experimental import pallas as pl
from jax.experimental.pallas import tpu as pltpu
from jax.sharding import PartitionSpec as P

NG = 256
LMAX = 8
LM = 81
KINDS = 3
ROWS = 256
CHUNK = 2048
GROUP = 16
HIGH = lax.Precision.HIGHEST
TWO_PI = 2.0 * math.pi
F32 = jnp.float32
BF16 = jnp.bfloat16
I32 = jnp.int32
PLANES_MB = 20
LAST_MB = 58


def norm(degree, m_order):
    base = (
        (2 * degree + 1)
        / (4 * math.pi)
        * math.factorial(degree - m_order)
        / math.factorial(degree + m_order)
    )
    return math.sqrt(base) * (math.sqrt(2.0) if m_order else 1.0)


def table_layout():
    tile_rows = [(d, 0) for d in range(1, 9)]
    tile_rows += [(8, m) for m in range(1, 9)] + [(8, -m) for m in range(1, 9)]
    tile_rows += [(4, r + 1) if r < 4 else (4, -(8 - r)) for r in range(8)]
    for low in (1, 2, 3):
        for sign in (1, -1):
            tile_rows += [
                (low, sign * (r + 1)) if r < low else (8 - low, sign * (8 - r)) for r in range(8)
            ]
    rows = {}
    for kind in range(KINDS):
        for at, (degree, m_order) in enumerate(tile_rows):
            rows[kind * 88 + at] = (kind, degree, m_order)
    rows[80] = (0, 0, 0)
    rows[168] = (1, 0, 0)
    rows[81] = (2, 0, 0)
    return rows


def placement_tables():
    spread = np.zeros((KINDS, 128, ROWS), np.float32)
    even = np.zeros((KINDS, ROWS, 128), np.float32)
    odd = np.zeros((KINDS, ROWS, 128), np.float32)
    for row, (kind, degree, m_order) in table_layout().items():
        lm = degree * degree + degree + m_order
        spread[kind, lm, row] = 1.0
        sign = -1.0 if degree % 4 in (1, 2) else 1.0
        (even if degree % 2 == 0 else odd)[kind, row, lm] = sign
    return spread, np.concatenate([even, odd], 0)


def recurrence_table():
    out = np.zeros((8, 128), np.float64)
    for direction in range(2):
        for r in range(8):
            m = r + 1 if direction == 0 else 8 - r
            start = float(np.prod(np.arange(1, 2 * m, 2)))
            for degree in range(1, 9):
                at = 3 * (8 * direction + degree - 1)
                if degree == m:
                    out[r, at + 2] = start * norm(m, m)
                elif degree > m:
                    out[r, at] = (
                        (2 * degree - 1) / (degree - m) * norm(degree, m) / norm(degree - 1, m)
                    )
                    if degree > m + 1:
                        out[r, at + 1] = (
                            (degree + m - 1) / (degree - m) * norm(degree, m) / norm(degree - 2, m)
                        )
    return out.astype(np.float32)


def fit_even(values, count):
    x = np.cos(np.pi * (np.arange(400) + 0.5) / 400) * 0.125 + 0.125
    basis = np.polynomial.chebyshev.Chebyshev.fit(x, values(np.sqrt(x)), count - 1, domain=[0, 0.25])
    return [float(c) for c in basis.convert(kind=np.polynomial.Polynomial, domain=[-1, 1]).coef]


SIN_FIT = fit_even(lambda x: np.sin(np.pi * x) / x, 5)
COS_FIT = fit_even(lambda x: np.cos(np.pi * x), 5)


def horner(coefficients, x):
    total = coefficients[-1]
    for coefficient in coefficients[-2::-1]:
        total = total * x + coefficient
    return total


def turn(t):
    t = t - jnp.floor(t + 0.5)
    square = t * t
    half_sin = t * horner(SIN_FIT, square)
    half_cos = horner(COS_FIT, square)
    return 1.0 - 2.0 * half_sin * half_sin, 2.0 * half_sin * half_cos


def split(x):
    high = x.astype(BF16)
    return high, (x - high.astype(F32)).astype(BF16)


def signed(index):
    return jnp.where(index >= NG // 2, index - NG, index).astype(F32)


def frequencies(position, owner, count):
    jx = (position >> 16) * count + owner
    jy = (position >> 8) & 255
    jz = position & 255
    return jx, signed(jx), signed(jy), signed(jz)


def table_of(freq, radial_ref, coef_ref, rows_scratch):
    freq_x, freq_y, freq_z = freq
    size_sq = freq_x * freq_x + freq_y * freq_y + freq_z * freq_z
    inv_size = 1.0 / jnp.sqrt(jnp.maximum(size_sq, 1.0))
    unit_x, unit_y, unit_z = freq_x * inv_size, freq_y * inv_size, freq_z * inv_size
    radius_sq = unit_x * unit_x + unit_y * unit_y + unit_z * unit_z
    width = unit_x.shape[1]
    cosine, sine = unit_x, unit_y
    for m in range(1, 9):
        rows_scratch[0, m - 1 : m, :] = cosine
        rows_scratch[1, m - 1 : m, :] = sine
        rows_scratch[2, 8 - m : 9 - m, :] = cosine
        rows_scratch[3, 8 - m : 9 - m, :] = sine
        cosine, sine = cosine * unit_x - sine * unit_y, sine * unit_x + cosine * unit_y
    before, current = jnp.zeros_like(unit_z), jnp.ones_like(unit_z)
    for degree in range(1, 9):
        before, current = (
            current,
            (2 * degree - 1) / degree * unit_z * current
            - (degree - 1) / degree * radius_sq * before,
        )
        rows_scratch[4, degree - 1 : degree, :] = norm(degree, 0) * current
    wide_z = jnp.broadcast_to(unit_z, (8, width))
    wide_sq = jnp.broadcast_to(radius_sq, (8, width))
    plain = []
    for direction in range(2):
        before = jnp.zeros((8, width), F32)
        current = jnp.zeros((8, width), F32)
        by_degree = [None]
        for degree in range(1, 9 - direction):
            at = 3 * (8 * direction + degree - 1)
            following = coef_ref[:, at + 2 : at + 3] + (coef_ref[:, at : at + 1] * wide_z) * current
            if degree > 2:
                following = following - (coef_ref[:, at + 1 : at + 2] * wide_sq) * before
            before, current = current, following
            by_degree.append(current)
        plain.append(by_degree)
    forward, reverse = plain
    cos_f, sin_f, cos_r, sin_r = (rows_scratch[i] for i in range(4))
    sub = lax.broadcasted_iota(I32, (8, width), 0)
    harm = [rows_scratch[4], forward[8] * cos_f, forward[8] * sin_f]
    harm.append(jnp.where(sub < 4, forward[4] * cos_f, reverse[4] * sin_r))
    for low in (1, 2, 3):
        harm.append(jnp.where(sub < low, forward[low] * cos_f, reverse[8 - low] * cos_r))
        harm.append(jnp.where(sub < low, forward[low] * sin_f, reverse[8 - low] * sin_r))
    zeros = jnp.zeros((8, width), F32)
    pieces = []
    first = norm(0, 0)
    for kind in range(KINDS):
        line = [
            jnp.broadcast_to(radial_ref[d, kind : kind + 1, :], (8, width)) for d in range(1, 9)
        ]
        line = [None] + line
        for d in range(1, 9):
            rows_scratch[5 + kind, d - 1 : d, :] = radial_ref[d, kind : kind + 1, :]
        pieces.append(harm[0] * rows_scratch[5 + kind])
        pieces.append(harm[1] * line[8])
        pieces.append(harm[2] * line[8])
        pieces.append(harm[3] * line[4])
        for low in (1, 2, 3):
            both = jnp.where(sub < low, line[low], line[8 - low])
            pieces.append(harm[2 + 2 * low] * both)
            pieces.append(harm[3 + 2 * low] * both)
        if kind < 2:
            own = jnp.broadcast_to(radial_ref[0, kind : kind + 1, :], (8, width)) * first
            extra = jnp.where(sub == 0, own, zeros)
            if kind == 0:
                third = jnp.broadcast_to(radial_ref[0, 2:3, :], (8, width)) * first
                extra = jnp.where(sub == 1, third, extra)
            pieces.append(extra)
    return split(jnp.concatenate(pieces, 0))


def angles(atoms_ref, freq):
    freq_x, freq_y, freq_z = freq
    return turn(
        atoms_ref[:, LM : LM + 1] * freq_x
        + atoms_ref[:, LM + 1 : LM + 2] * freq_y
        + atoms_ref[:, LM + 2 : LM + 3] * freq_z
    )


def gather_kernel(
    count, place_ref, moments_ref, positions_ref, species_ref, index_ref, out_ref, key_ref, held
):
    own = moments_ref.shape[0]
    lane = lax.broadcasted_iota(I32, (own, 128), 1)
    diagonal = lax.broadcasted_iota(I32, (own, own), 0) == lax.broadcasted_iota(I32, (own, own), 1)
    total = jnp.zeros((own, 128), F32)
    rows = [positions_ref[c : c + 1, :] for c in range(3)] + [species_ref[...].astype(F32)]
    for c, row in enumerate(rows):
        spread = jnp.where(diagonal, jnp.broadcast_to(row, (own, own)), 0.0)
        column = jnp.sum(spread, axis=1, keepdims=True)
        total = jnp.where(lane == LM + c, column, total)
    held[...] = total
    held[:, 0:LM] = moments_ref[...]
    out_ref[...] = jnp.broadcast_to(held[...][None], out_ref.shape)
    index = index_ref[...]
    jx = (index >> 16) * count + place_ref[0]
    jy = (index >> 8) & 255
    jz = index & 255
    folded = jnp.where(jx > NG // 2, ((-jy & 255) << 8) | (-jz & 255), (jy << 8) | jz)
    key_ref[...] = ((index >> 16) << 16) | folded


def charge_kernel(
    count,
    place_ref,
    atoms_ref,
    spread_ref,
    coef_ref,
    radial_ref,
    inter_ref,
    index_ref,
    key_ref,
    order_ref,
    pot_ref,
    sent_ref,
    cos_ref,
    sin_ref,
    weights,
    rows_scratch,
    values,
):
    step = pl.program_id(0)
    atoms = atoms_ref.shape[0]
    per_chunk = CHUNK // 128

    @pl.when(step == 0)
    def _():
        kind = atoms_ref[:, LM + 3 : LM + 4]
        total = jnp.zeros((atoms, ROWS), F32)
        for s in range(KINDS):
            moved = jnp.dot(
                atoms_ref[...], spread_ref[s], precision=HIGH, preferred_element_type=F32
            )
            total = total + jnp.where(kind == float(s), moved, 0.0)
        high, low = split(total)
        weights[0:atoms, :] = high
        weights[atoms : 2 * atoms, :] = low

    jx, *freq = frequencies(index_ref[...], place_ref[0], count)
    table_high, table_low = table_of(freq, radial_ref, coef_ref, rows_scratch)
    main = jnp.dot(weights[...], table_high, preferred_element_type=F32)
    rest = jnp.dot(weights[0:atoms, :], table_low, preferred_element_type=F32)
    shape_part = main[0:atoms] + (main[atoms:] + rest)
    cosine, sine = angles(atoms_ref, freq)
    cos_ref[...] = cosine
    sin_ref[...] = sine
    pseudo_re = jnp.sum(shape_part * cosine, axis=0, keepdims=True)
    pseudo_im = -jnp.sum(shape_part * sine, axis=0, keepdims=True)
    freq_x, freq_y, freq_z = freq
    size_sq = freq_x * freq_x + freq_y * freq_y + freq_z * freq_z
    kernel = jnp.where(size_sq > 0, 1.0 / jnp.maximum(size_sq, 1.0), 0.0)
    pot_re = (inter_ref[0:1, :] + pseudo_re) * kernel
    pot_im = (inter_ref[1:2, :] + pseudo_im) * kernel
    pot_ref[0:1, :] = pot_re
    pot_ref[1:2, :] = pot_im
    folded_im = jnp.where(jx > NG // 2, -pot_im, pot_im)
    for j in range(per_chunk):
        line = pl.ds(step * per_chunk + j, 1)
        values[0, line, :] = pot_re[:, j * 128 : (j + 1) * 128]
        values[1, line, :] = folded_im[:, j * 128 : (j + 1) * 128]

    @pl.when(step == pl.num_programs(0) - 1)
    def _():
        order = order_ref[...]
        lines = order.shape[0]
        lane = order & 127
        line_of = order >> 7

        def one_line(r, carried):
            taken_re, taken_im = carried
            here = line_of == r
            row_re = jnp.broadcast_to(values[0, pl.ds(r, 1), :], (lines, 128))
            row_im = jnp.broadcast_to(values[1, pl.ds(r, 1), :], (lines, 128))
            taken_re = jnp.where(here, jnp.take_along_axis(row_re, lane, 1, mode="promise_in_bounds"), taken_re)
            taken_im = jnp.where(here, jnp.take_along_axis(row_im, lane, 1, mode="promise_in_bounds"), taken_im)
            return taken_re, taken_im

        empty = jnp.zeros((lines, 128), F32)
        taken_re, taken_im = lax.fori_loop(0, lines, one_line, (empty, empty), unroll=8)
        key = key_ref[...]
        sent_ref[0:lines, :] = taken_re
        sent_ref[lines : 2 * lines, :] = taken_im
        sent_ref[2 * lines : 3 * lines, :] = key.astype(F32)
        begins = (lax.broadcasted_iota(I32, (8, 128), 1) * 256).astype(F32)
        ends = begins + 255.0
        first = jnp.zeros((8, 128), F32)
        last = jnp.zeros((8, 128), F32)
        for k in range(1, NG // count):
            below = jnp.sum((key < (k << 16)).astype(F32), axis=(0, 1), keepdims=True)
            first = first + jnp.where(below <= begins, 1.0, 0.0)
            last = last + jnp.where(below <= ends, 1.0, 0.0)
        sub = lax.broadcasted_iota(I32, (8, 128), 0)
        sent_ref[3 * lines :, :] = jnp.where(sub == 0, first, last)


def boundary_kernel(
    count,
    place_ref,
    atoms_ref,
    gather_ref,
    coef_ref,
    slot_ref,
    bessel_ref,
    pot_ref,
    index_ref,
    cos_ref,
    sin_ref,
    out_ref,
    total,
    rows_scratch,
):
    step = pl.program_id(0)
    atoms = atoms_ref.shape[0]
    _, *freq = frequencies(index_ref[...], place_ref[0], count)
    table_high, table_low = table_of(freq, bessel_ref, coef_ref, rows_scratch)
    cosine, sine = cos_ref[...], sin_ref[...]
    pot_re, pot_im = pot_ref[0:1, :], pot_ref[1:2, :]
    real_part = pot_re * cosine - pot_im * sine
    imag_part = pot_re * sine + pot_im * cosine
    high, low = split(jnp.concatenate([real_part, imag_part], 0))
    dims = (((1,), (1,)), ((), ()))
    both = lax.dot_general(
        jnp.concatenate([high, low], 0), table_high, dims, preferred_element_type=F32
    )
    rest = lax.dot_general(high, table_low, dims, preferred_element_type=F32)
    add = both[0 : 2 * atoms] + (both[2 * atoms :] + rest)

    @pl.when(step == 0)
    def _():
        total[...] = add

    @pl.when(step > 0)
    def _():
        total[...] += add

    @pl.when(step == pl.num_programs(0) - 1)
    def _():
        kind = atoms_ref[:, LM + 3 : LM + 4]
        raw = jnp.zeros((atoms, 128), F32)
        for s in range(KINDS):
            part = jnp.dot(
                total[0:atoms, :], gather_ref[s], precision=HIGH, preferred_element_type=F32
            ) + jnp.dot(
                total[atoms:, :], gather_ref[KINDS + s], precision=HIGH, preferred_element_type=F32
            )
            raw = raw + jnp.where(kind == float(s), part, 0.0)
        slots = lax.broadcasted_iota(I32, (atoms, atoms), 0)
        moved = (slots == slot_ref[...]).astype(F32)
        out_ref[...] = jnp.dot(moved, raw, precision=HIGH, preferred_element_type=F32)


def plane_type(place):
    return ((place >> 1) ^ ((place & 1) * (place >> 2))) & 1


def planes_kernel(count, pattern, *refs):
    place_ref, recv_ref, step_ref, own_out, other_out = refs[:5]
    own_ref, other_ref, wave, start_ref, sem, store_sem = refs[5:11]
    box, front, back, fields = refs[11:]
    rows = NG // count
    chip_rows = 2 * rows
    sources = recv_ref.shape[0]
    lines = (recv_ref.shape[1] - 8) // 3
    halves = 1 if pattern is None else 2
    local_planes = NG // 4 // halves
    pitch = 2 * GROUP + 8
    tiles = lines // 2
    together = math.gcd(tiles, 16)
    place = place_ref[0]
    core = place % 2
    base = (place // 2) * chip_rows

    fetch = pltpu.make_async_copy(recv_ref.at[:, pl.ds(3 * lines, 8), :], start_ref, sem.at[0])
    fetch.start()
    box[...] = jnp.zeros_like(box)

    sub = lax.broadcasted_iota(I32, (8, 128), 0)
    if chip_rows == 8:
        start_rows = (base + (sub + core * rows) % chip_rows).astype(F32) * (1.0 / NG)
    else:
        start_rows = (base + core * rows + sub).astype(F32) * (1.0 / NG)
    across = (1 - 2 * core).astype(F32) * (rows / NG)

    def all_fields(s, _):
        keys = recv_ref[s, 2 * lines : 3 * lines, :].astype(I32)
        jy = ((keys >> 8) & 255).astype(F32)
        fields[s, 0] = jy
        fields[s, 1] = (keys & 255).astype(F32)
        fields[s, 2] = (keys >> 16).astype(F32)
        if chip_rows > 8:
            fields[s, 3], fields[s, 4] = turn(jy * (8.0 / NG))
            fields[s, 5], fields[s, 6] = turn(jy * across)
        return 0

    lax.fori_loop(0, sources, all_fields, 0)

    def one_chunk(s, i, held):
        v_re = recv_ref[s, pl.ds(i, 1), :]
        v_im = recv_ref[s, pl.ds(lines + i, 1), :]
        jy, c_step, s_step, c_far, s_far = (
            fields[s, f, pl.ds(i, 1), :] if f == 0 or chip_rows > 8 else None
            for f in (0, 3, 4, 5, 6)
        )
        c, s = turn(jnp.broadcast_to(jy, (8, 128)) * start_rows)
        parts = [(v_re * c - v_im * s, v_re * s + v_im * c)]
        if chip_rows > 8:
            while 8 * len(parts) < rows:
                re, im = parts[-1]
                parts.append((re * c_step - im * s_step, re * s_step + im * c_step))
            parts += [(re * c_far - im * s_far, re * s_far + im * c_far) for re, im in parts]
        high, low = split(jnp.concatenate([re for re, _ in parts] + [im for _, im in parts], 0))
        held[i] = jnp.concatenate([high, low], 0)

    def edge(s, t, which):
        return start_ref[s, which, t].astype(I32)

    def plane_at(s, k):
        if pattern is None:
            owner = 2 * s + core
        else:
            owner = place ^ pattern ^ (8 * (s >> 1) + (4 + 2 * core) * (s & 1))
        jx = k * count + owner
        return jnp.where(jx > NG // 2, NG - jx, jx) // (2 * halves)

    def add_tile(s, t, wanted, held):
        left, right = [], []
        for i in (2 * t, 2 * t + 1):
            spot = jnp.broadcast_to(fields[s, 1, pl.ds(i, 1), :], (16, 128)).astype(BF16)
            hits = [
                jnp.where(
                    step_ref[16 * r : 16 * r + 16, :] == spot,
                    jnp.ones((16, 128), BF16),
                    jnp.zeros((16, 128), BF16),
                )
                for r in range(NG // 16)
            ]
            right.append(jnp.concatenate(hits, 0))
            plane = jnp.broadcast_to(fields[s, 2, pl.ds(i, 1), :], (16, 128))
            phased = held[i]
            masked = []
            for k, used in wanted:
                mask = jnp.where(plane == k.astype(F32), used, 0.0).astype(BF16)
                masked.append(phased * jnp.concatenate([mask] * (phased.shape[0] // 16), 0))
            left.append(jnp.concatenate(masked, 0))
        out = lax.dot_general(
            jnp.concatenate(left, 1),
            jnp.concatenate(right, 1),
            (((1,), (1,)), ((), ())),
            preferred_element_type=F32,
        )
        size = 2 * chip_rows
        for j, (k, _) in enumerate(wanted):
            box[plane_at(s, k)] += (
                out[2 * j * size : (2 * j + 1) * size] + out[(2 * j + 1) * size : (2 * j + 2) * size]
            )

    def one_source(s, held, following, filled):
        def some_tiles(g, most):
            for j in range(together):
                t = g * together + j
                first, last = edge(s, t, 0), edge(s, t, 1)
                second = jnp.where(last > first, 1.0, 0.0)
                add_tile(s, t, [(first, 1.0), (last, second)], held)
                if filled is not None:
                    one_chunk(following, 2 * t, filled)
                    one_chunk(following, 2 * t + 1, filled)
                most = jnp.maximum(most, last - first)
            return most

        most = lax.fori_loop(0, tiles // together, some_tiles, jnp.int32(0))

        @pl.when(most > 1)
        def _():
            def one_tile(t, _):
                def between(k, _):
                    add_tile(s, t, [(k, 1.0)], held)
                    return 0

                return lax.fori_loop(edge(s, t, 0) + 1, edge(s, t, 1), between, 0)

            lax.fori_loop(0, tiles, one_tile, 0)

    def first_chunks(g, _):
        for j in range(8):
            one_chunk(0, 8 * g + j, front)
        return 0

    lax.fori_loop(0, lines // 8, first_chunks, 0)
    fetch.wait()

    def two_sources(t, _):
        one_source(2 * t, front, 2 * t + 1, back)
        one_source(2 * t + 1, back, 2 * t + 2, front)
        return 0

    lax.fori_loop(0, sources // 2 - 1, two_sources, 0)
    one_source(sources - 2, front, sources - 1, back)
    one_source(sources - 1, back, None, None)
    grid = [lax.broadcasted_iota(I32, (NG, NG), d).astype(F32) for d in range(2)]
    cos_z, sin_z = turn(grid[0] * grid[1] * (1.0 / NG))
    for j, table in enumerate(([cos_z, sin_z], [-sin_z, cos_z])):
        high, low = split(jnp.concatenate(table, 1))
        for k, part in enumerate((high, high, low)):
            wave[(3 * j + k) * NG : (3 * j + k + 1) * NG, :] = part

    def along_z(at, number):
        block = box[pl.ds(at, number)]
        left = []
        for part in (block[:, :chip_rows], block[:, chip_rows:]):
            high, low = split(part.reshape(number * chip_rows, NG))
            left += [high, low, high]
        out = jnp.dot(jnp.concatenate(left, 1), wave[...], preferred_element_type=F32)
        out = out.reshape(number, chip_rows, 2 * NG)
        return out[:, :, :NG], out[:, :, NG:]

    def keep(g, at, value):
        line = pl.ds(at, rows, stride=pitch)
        for h in range(2):
            own_ref[g, h, line, :] = value[:rows, h * 128 : (h + 1) * 128]
            other_ref[g, h, line, :] = value[rows:, h * 128 : (h + 1) * 128]

    has_middle = core == 0
    if pattern is not None:
        has_middle = has_middle & (plane_type(place) == (1 if pattern else 0))
    stores = []
    for g in range(local_planes // GROUP):
        re, im = along_z(g * GROUP, GROUP)
        for j in range(GROUP):
            keep(g, 2 * j, re[j])
            keep(g, 2 * j + 1, im[j])
        if g == 0:

            @pl.when(has_middle)
            def _():
                re, _ = along_z(local_planes, 1)
                keep(0, 1, re[0])

        for j, (made, out) in enumerate(((other_ref, other_out), (own_ref, own_out))):
            stores.append(pltpu.make_async_copy(made.at[g], out.at[g], store_sem.at[g, j]))
            stores[-1].start()
    for store in stores:
        store.wait()


def planes_call(count, place, recv, pattern, steps):
    rows = NG // count
    sources = recv.shape[0]
    lines = (recv.shape[1] - 8) // 3
    local_planes = NG // 4 // (1 if pattern is None else 2)
    groups = local_planes // GROUP
    half = jax.ShapeDtypeStruct((groups, 2, rows * (2 * GROUP + 8), 128), F32)
    vmem = pl.BlockSpec(memory_space=pltpu.VMEM)
    anywhere = pl.BlockSpec(memory_space=pltpu.HBM)
    held = pltpu.VMEM((lines, 8 * rows, 128), BF16)
    return pl.pallas_call(
        functools.partial(planes_kernel, count, pattern),
        in_specs=[smem(), vmem, vmem],
        out_specs=[anywhere, anywhere],
        out_shape=[half, half],
        scratch_shapes=[
            pltpu.VMEM(half.shape, F32),
            pltpu.VMEM(half.shape, F32),
            pltpu.VMEM((6 * NG, 2 * NG), BF16),
            pltpu.SMEM((sources, 8, 128), F32),
            pltpu.SemaphoreType.DMA((2,)),
            pltpu.SemaphoreType.DMA((groups, 2)),
            pltpu.VMEM((local_planes + 1, 4 * rows, NG), F32),
            held,
            held,
            pltpu.VMEM((sources, 7, lines, 128), F32),
        ],
        compiler_params=params(PLANES_MB),
        name="planes_far" if pattern else "planes_near",
        cost_estimate=cost(15),
    )(place, recv, steps)


def last_kernel(count, place_ref, wave_ref, *refs):
    halves = (len(refs) - 6) // 2
    given = refs[: 2 * halves]
    out_ref, held, wave, tables_ref, parts, sem = refs[2 * halves :]
    rows = NG // count
    pitch = 2 * GROUP + 8
    place = place_ref[0]
    group = 4
    fetch_tables = pltpu.make_async_copy(wave_ref, tables_ref, sem.at[0, 2 * halves])
    fetch_tables.start()
    fetches = []
    for g in range(rows // group):
        line = pl.ds(g * group * pitch, group * pitch)
        fetches.append(
            [
                pltpu.make_async_copy(
                    part.at[:, :, line, :], parts.at[i, :, :, line, :], sem.at[g, i]
                )
                for i, part in enumerate(given)
            ]
        )
        for fetch in fetches[-1]:
            fetch.start()
    fetch_tables.wait()
    tables = []
    for device in (place, place ^ 1):
        for half in range(halves):
            which = device & 1
            if halves == 2:
                which = 2 * which + (plane_type(device) ^ half)
            tables.append(tables_ref[which])
    wave[0], wave[1] = split(jnp.concatenate(tables, 0).T)

    def one_row(y):
        line = pl.ds(y * pitch, 2 * GROUP)
        mixed = [
            jnp.concatenate(
                [parts[i, q, h, line, :] for i in range(2 * halves) for q in range(parts.shape[1])],
                0,
            )
            for h in range(2)
        ]
        high, low = split(jnp.concatenate(mixed, 1))
        main = jnp.dot(wave[...].reshape(2 * NG, NG), high, preferred_element_type=F32)
        rest = jnp.dot(wave[0], low, preferred_element_type=F32)
        out = main[:NG] + (main[NG:] + rest)
        for h in range(2):
            held[h, pl.ds(y, NG, stride=rows), :] = out[:, h * 128 : (h + 1) * 128]

    for g in range(rows // group):
        for fetch in fetches[g]:
            fetch.wait()
        for y in range(g * group, (g + 1) * group):
            one_row(y)
    copies = [
        pltpu.make_async_copy(held.at[h], out_ref.at[:, pl.ds(h * 128, 128)], sem.at[0, h])
        for h in range(2)
    ]
    for copy in copies:
        copy.start()
    for copy in copies:
        copy.wait()


def wave_tables(halves):
    j = np.arange(NG)
    along_x = []
    for core in range(2):
        for kind in range(halves):
            planes = np.arange(core, NG // 2, 2)
            if halves == 2 and core == 0:
                planes = planes[planes % 4 == 2 * kind]
            elif halves == 2:
                planes = planes[np.isin(planes % 8, (3, 5) if kind else (1, 7))]
            phase = 2 * np.pi / NG * ((planes[:, None] * j[None, :]) % NG)
            table = np.stack([np.cos(phase), -np.sin(phase)], 1).reshape(-1, NG)
            if planes[0] == 0:
                table[1] = np.cos(np.pi * j)
            along_x.append(table)
    return np.stack(along_x).astype(np.float32)


def smem():
    return pl.BlockSpec(memory_space=pltpu.SMEM)


def cost(micros):
    return pl.CostEstimate(flops=int(micros * 1e9), bytes_accessed=0, transcendentals=0)


def params(megabytes=56):
    return pltpu.CompilerParams(vmem_limit_bytes=megabytes * 1024 * 1024)


def body(
    multipoles, positions, species, atom_slot, pseudo_radial, boundary_bessel, interstitial, g_index
):
    count = lax.axis_size("pencil")
    owner = lax.axis_index("pencil").astype(I32)
    place = owner.reshape(1)
    local_g = g_index.shape[0]
    lines = local_g // 128
    chunks = local_g // CHUNK
    atoms = atom_slot.shape[0]
    own_atoms = multipoles.shape[1]
    rows = NG // count
    spread, gather = placement_tables()
    coef = jnp.asarray(recurrence_table())
    along_x = wave_tables(2 if count == 16 else 1)

    vmem = pl.BlockSpec(memory_space=pltpu.VMEM)
    copies, key = pl.pallas_call(
        functools.partial(gather_kernel, count),
        in_specs=[smem(), vmem, vmem, vmem, vmem],
        out_specs=[vmem, vmem],
        out_shape=[
            jax.ShapeDtypeStruct((count, own_atoms, 128), F32),
            jax.ShapeDtypeStruct((lines, 128), I32),
        ],
        scratch_shapes=[pltpu.VMEM((own_atoms, 128), F32)],
        compiler_params=params(),
        name="atoms",
    )(
        place,
        multipoles.T,
        positions,
        species.reshape(1, own_atoms),
        g_index.reshape(lines, 128),
    )
    atom_rows = lax.all_to_all(copies, "pencil", split_axis=0, concat_axis=0, tiled=True)
    atom_rows = atom_rows.reshape(atoms, 128)

    key, order = lax.sort(
        (key.reshape(local_g), lax.iota(I32, local_g)), num_keys=1, is_stable=False
    )
    key = key.reshape(lines, 128)
    order = order.reshape(lines, 128)
    index_line = g_index.reshape(1, local_g)

    whole = lambda a: pl.BlockSpec(a.shape, lambda i: (0,) * a.ndim)
    line_spec = pl.BlockSpec((1, CHUNK), lambda i: (0, i))
    pair_spec = pl.BlockSpec((2, CHUNK), lambda i: (0, i))
    radial_spec = pl.BlockSpec((LMAX + 1, KINDS, CHUNK), lambda i: (0, 0, i))
    spread = jnp.asarray(spread)
    atom_spec = pl.BlockSpec((atoms, CHUNK), lambda i: (0, i))
    pot, sent, cosine, sine = pl.pallas_call(
        functools.partial(charge_kernel, count),
        grid=(chunks,),
        in_specs=[
            smem(),
            whole(atom_rows),
            whole(spread),
            whole(coef),
            radial_spec,
            pair_spec,
            line_spec,
            whole(key),
            whole(order),
        ],
        out_specs=[
            pair_spec,
            pl.BlockSpec((3 * lines + 8, 128), lambda i: (0, 0)),
            atom_spec,
            atom_spec,
        ],
        out_shape=[
            jax.ShapeDtypeStruct((2, local_g), F32),
            jax.ShapeDtypeStruct((3 * lines + 8, 128), F32),
            jax.ShapeDtypeStruct((atoms, local_g), F32),
            jax.ShapeDtypeStruct((atoms, local_g), F32),
        ],
        scratch_shapes=[
            pltpu.VMEM((2 * atoms, ROWS), BF16),
            pltpu.VMEM((8, 8, CHUNK), F32),
            pltpu.VMEM((2, lines, 128), F32),
        ],
        compiler_params=params(),
        name="charge",
        cost_estimate=cost(10),
    )(place, atom_rows, spread, coef, pseudo_radial.transpose(1, 0, 2), interstitial, index_line, key, order)

    gather = jnp.asarray(gather)
    slot_line = atom_slot.reshape(1, atoms)
    partial_raw = pl.pallas_call(
        functools.partial(boundary_kernel, count),
        grid=(chunks,),
        in_specs=[
            smem(),
            whole(atom_rows),
            whole(gather),
            whole(coef),
            whole(slot_line),
            radial_spec,
            pair_spec,
            line_spec,
            atom_spec,
            atom_spec,
        ],
        out_specs=pl.BlockSpec((atoms, 128), lambda i: (0, 0)),
        out_shape=jax.ShapeDtypeStruct((atoms, 128), F32),
        scratch_shapes=[
            pltpu.VMEM((2 * atoms, ROWS), F32),
            pltpu.VMEM((8, 8, CHUNK), F32),
        ],
        compiler_params=params(),
        name="boundary",
        cost_estimate=cost(10),
    )(place, atom_rows, gather, coef, slot_line, boundary_bessel.transpose(1, 0, 2), pot, index_line, cosine, sine)
    parts = lax.all_to_all(partial_raw, "pencil", split_axis=0, concat_axis=0, tiled=True)

    steps = jnp.asarray(np.broadcast_to(np.arange(NG)[:, None], (NG, 128)).astype(BF16))
    sibling = [(i, i ^ 1) for i in range(count)]
    if count == 16:
        masks = [lambda i: 4 + 2 * (i & 1), lambda i: 8, lambda i: 12 + 2 * (i & 1)]
        pieces = [
            lax.ppermute(sent, "pencil", [(i, i ^ mask(i)) for i in range(count)])
            for mask in masks
        ]
        pieces, partial_raw = lax.optimization_barrier((pieces, partial_raw))
        near = jnp.stack([sent] + pieces)
        far = lax.ppermute(near, "pencil", [(i, i ^ 2) for i in range(count)])
        own_near, other_near = planes_call(count, place, near, 0, steps)
        other_near = lax.ppermute(other_near, "pencil", sibling)
        far, parts = lax.optimization_barrier((far, parts))
        own_far, other_far = planes_call(count, place, far, 2, steps)
        other_far = lax.ppermute(other_far, "pencil", sibling)
        waves = [own_near, own_far, other_near, other_far]
    else:
        groups = [list(range(c, count, 2)) for c in range(2)]
        recv = lax.all_gather(sent, "pencil", axis_index_groups=groups)
        own, other = planes_call(count, place, recv, None, steps)
        waves = [own, lax.ppermute(other, "pencil", sibling)]

    boundary = jnp.sum(parts.reshape(count, own_atoms, 128), axis=0)[:, :LM].T
    along_x = jnp.asarray(along_x)
    anywhere = pl.BlockSpec(memory_space=pltpu.HBM)
    potential = pl.pallas_call(
        functools.partial(last_kernel, count),
        in_specs=[smem()] + [anywhere] * (1 + len(waves)),
        out_specs=anywhere,
        out_shape=jax.ShapeDtypeStruct((NG * rows, NG), F32),
        scratch_shapes=[
            pltpu.VMEM((2, NG * rows, 128), F32),
            pltpu.VMEM((2, NG, NG), BF16),
            pltpu.VMEM(along_x.shape, F32),
            pltpu.VMEM((len(waves),) + waves[0].shape, F32),
            pltpu.SemaphoreType.DMA((rows // 4, 5)),
        ],
        compiler_params=params(LAST_MB),
        name="last",
        cost_estimate=cost(7),
    )(place, along_x, *waves)
    return (potential.reshape(NG, rows, NG), boundary)


def solution(mesh):
    placed = (
        P(None, ("cells", "pencil")),
        P(None, ("cells", "pencil")),
        P(("cells", "pencil")),
        P("cells"),
        P(None, None, ("cells", "pencil")),
        P(None, None, ("cells", "pencil")),
        P(None, ("cells", "pencil")),
        P(("cells", "pencil")),
    )
    return jax.shard_map(
        body,
        mesh=mesh,
        in_specs=placed,
        out_specs=(P("cells", "pencil", None), P(None, ("cells", "pencil"))),
        check_vma=False,
    )
```

```python
import functools
import math

import jax
import jax.numpy as jnp
import numpy as np
from jax import lax
from jax.experimental import pallas as pl
from jax.experimental.pallas import tpu as pltpu
from jax.sharding import PartitionSpec as P

NG = 256
LMAX = 8
LM = 81
KINDS = 3
ROWS = 256
CHUNK = 2048
GROUP = 16
HIGH = lax.Precision.HIGHEST
TWO_PI = 2.0 * math.pi
F32 = jnp.float32
BF16 = jnp.bfloat16
I32 = jnp.int32
PLANES_MB = 20
LAST_MB = 58


def norm(degree, m_order):
    base = (
        (2 * degree + 1)
        / (4 * math.pi)
        * math.factorial(degree - m_order)
        / math.factorial(degree + m_order)
    )
    return math.sqrt(base) * (math.sqrt(2.0) if m_order else 1.0)


def table_layout():
    tile_rows = [(d, 0) for d in range(1, 9)]
    tile_rows += [(8, m) for m in range(1, 9)] + [(8, -m) for m in range(1, 9)]
    tile_rows += [(4, r + 1) if r < 4 else (4, -(8 - r)) for r in range(8)]
    for low in (1, 2, 3):
        for sign in (1, -1):
            tile_rows += [
                (low, sign * (r + 1)) if r < low else (8 - low, sign * (8 - r)) for r in range(8)
            ]
    rows = {}
    for kind in range(KINDS):
        for at, (degree, m_order) in enumerate(tile_rows):
            rows[kind * 88 + at] = (kind, degree, m_order)
    rows[80] = (0, 0, 0)
    rows[168] = (1, 0, 0)
    rows[81] = (2, 0, 0)
    return rows


def placement_tables():
    spread = np.zeros((KINDS, 128, ROWS), np.float32)
    even = np.zeros((KINDS, ROWS, 128), np.float32)
    odd = np.zeros((KINDS, ROWS, 128), np.float32)
    for row, (kind, degree, m_order) in table_layout().items():
        lm = degree * degree + degree + m_order
        spread[kind, lm, row] = 1.0
        sign = -1.0 if degree % 4 in (1, 2) else 1.0
        (even if degree % 2 == 0 else odd)[kind, row, lm] = sign
    return spread, np.concatenate([even, odd], 0)


def recurrence_table():
    out = np.zeros((8, 128), np.float64)
    for direction in range(2):
        for r in range(8):
            m = r + 1 if direction == 0 else 8 - r
            start = float(np.prod(np.arange(1, 2 * m, 2)))
            for degree in range(1, 9):
                at = 3 * (8 * direction + degree - 1)
                if degree == m:
                    out[r, at + 2] = start * norm(m, m)
                elif degree > m:
                    out[r, at] = (
                        (2 * degree - 1) / (degree - m) * norm(degree, m) / norm(degree - 1, m)
                    )
                    if degree > m + 1:
                        out[r, at + 1] = (
                            (degree + m - 1) / (degree - m) * norm(degree, m) / norm(degree - 2, m)
                        )
    return out.astype(np.float32)


def fit_even(values, count):
    x = np.cos(np.pi * (np.arange(400) + 0.5) / 400) * 0.125 + 0.125
    basis = np.polynomial.chebyshev.Chebyshev.fit(x, values(np.sqrt(x)), count - 1, domain=[0, 0.25])
    return [float(c) for c in basis.convert(kind=np.polynomial.Polynomial, domain=[-1, 1]).coef]


SIN_FIT = fit_even(lambda x: np.sin(np.pi * x) / x, 5)
COS_FIT = fit_even(lambda x: np.cos(np.pi * x), 5)


def horner(coefficients, x):
    total = coefficients[-1]
    for coefficient in coefficients[-2::-1]:
        total = total * x + coefficient
    return total


def turn(t):
    t = t - jnp.floor(t + 0.5)
    square = t * t
    half_sin = t * horner(SIN_FIT, square)
    half_cos = horner(COS_FIT, square)
    return 1.0 - 2.0 * half_sin * half_sin, 2.0 * half_sin * half_cos


def split(x):
    high = x.astype(BF16)
    return high, (x - high.astype(F32)).astype(BF16)


def signed(index):
    return jnp.where(index >= NG // 2, index - NG, index).astype(F32)


def frequencies(position, owner, count):
    jx = (position >> 16) * count + owner
    jy = (position >> 8) & 255
    jz = position & 255
    return jx, signed(jx), signed(jy), signed(jz)


def table_of(freq, radial_ref, coef_ref, rows_scratch):
    freq_x, freq_y, freq_z = freq
    size_sq = freq_x * freq_x + freq_y * freq_y + freq_z * freq_z
    inv_size = 1.0 / jnp.sqrt(jnp.maximum(size_sq, 1.0))
    unit_x, unit_y, unit_z = freq_x * inv_size, freq_y * inv_size, freq_z * inv_size
    radius_sq = unit_x * unit_x + unit_y * unit_y + unit_z * unit_z
    width = unit_x.shape[1]
    cosine, sine = unit_x, unit_y
    for m in range(1, 9):
        rows_scratch[0, m - 1 : m, :] = cosine
        rows_scratch[1, m - 1 : m, :] = sine
        rows_scratch[2, 8 - m : 9 - m, :] = cosine
        rows_scratch[3, 8 - m : 9 - m, :] = sine
        cosine, sine = cosine * unit_x - sine * unit_y, sine * unit_x + cosine * unit_y
    before, current = jnp.zeros_like(unit_z), jnp.ones_like(unit_z)
    for degree in range(1, 9):
        before, current = (
            current,
            (2 * degree - 1) / degree * unit_z * current
            - (degree - 1) / degree * radius_sq * before,
        )
        rows_scratch[4, degree - 1 : degree, :] = norm(degree, 0) * current
    wide_z = jnp.broadcast_to(unit_z, (8, width))
    wide_sq = jnp.broadcast_to(radius_sq, (8, width))
    plain = []
    for direction in range(2):
        before = jnp.zeros((8, width), F32)
        current = jnp.zeros((8, width), F32)
        by_degree = [None]
        for degree in range(1, 9 - direction):
            at = 3 * (8 * direction + degree - 1)
            following = coef_ref[:, at + 2 : at + 3] + (coef_ref[:, at : at + 1] * wide_z) * current
            if degree > 2:
                following = following - (coef_ref[:, at + 1 : at + 2] * wide_sq) * before
            before, current = current, following
            by_degree.append(current)
        plain.append(by_degree)
    forward, reverse = plain
    cos_f, sin_f, cos_r, sin_r = (rows_scratch[i] for i in range(4))
    sub = lax.broadcasted_iota(I32, (8, width), 0)
    harm = [rows_scratch[4], forward[8] * cos_f, forward[8] * sin_f]
    harm.append(jnp.where(sub < 4, forward[4] * cos_f, reverse[4] * sin_r))
    for low in (1, 2, 3):
        harm.append(jnp.where(sub < low, forward[low] * cos_f, reverse[8 - low] * cos_r))
        harm.append(jnp.where(sub < low, forward[low] * sin_f, reverse[8 - low] * sin_r))
    zeros = jnp.zeros((8, width), F32)
    pieces = []
    first = norm(0, 0)
    for kind in range(KINDS):
        line = [
            jnp.broadcast_to(radial_ref[d, kind : kind + 1, :], (8, width)) for d in range(1, 9)
        ]
        line = [None] + line
        for d in range(1, 9):
            rows_scratch[5 + kind, d - 1 : d, :] = radial_ref[d, kind : kind + 1, :]
        pieces.append(harm[0] * rows_scratch[5 + kind])
        pieces.append(harm[1] * line[8])
        pieces.append(harm[2] * line[8])
        pieces.append(harm[3] * line[4])
        for low in (1, 2, 3):
            both = jnp.where(sub < low, line[low], line[8 - low])
            pieces.append(harm[2 + 2 * low] * both)
            pieces.append(harm[3 + 2 * low] * both)
        if kind < 2:
            own = jnp.broadcast_to(radial_ref[0, kind : kind + 1, :], (8, width)) * first
            extra = jnp.where(sub == 0, own, zeros)
            if kind == 0:
                third = jnp.broadcast_to(radial_ref[0, 2:3, :], (8, width)) * first
                extra = jnp.where(sub == 1, third, extra)
            pieces.append(extra)
    return split(jnp.concatenate(pieces, 0))


def angles(atoms_ref, freq):
    freq_x, freq_y, freq_z = freq
    return turn(
        atoms_ref[:, LM : LM + 1] * freq_x
        + atoms_ref[:, LM + 1 : LM + 2] * freq_y
        + atoms_ref[:, LM + 2 : LM + 3] * freq_z
    )


def gather_kernel(
    count, place_ref, moments_ref, positions_ref, species_ref, index_ref, out_ref, key_ref, held
):
    own = moments_ref.shape[0]
    lane = lax.broadcasted_iota(I32, (own, 128), 1)
    diagonal = lax.broadcasted_iota(I32, (own, own), 0) == lax.broadcasted_iota(I32, (own, own), 1)
    total = jnp.zeros((own, 128), F32)
    rows = [positions_ref[c : c + 1, :] for c in range(3)] + [species_ref[...].astype(F32)]
    for c, row in enumerate(rows):
        spread = jnp.where(diagonal, jnp.broadcast_to(row, (own, own)), 0.0)
        column = jnp.sum(spread, axis=1, keepdims=True)
        total = jnp.where(lane == LM + c, column, total)
    held[...] = total
    held[:, 0:LM] = moments_ref[...]
    out_ref[...] = jnp.broadcast_to(held[...][None], out_ref.shape)
    index = index_ref[...]
    jx = (index >> 16) * count + place_ref[0]
    jy = (index >> 8) & 255
    jz = index & 255
    folded = jnp.where(jx > NG // 2, ((-jy & 255) << 8) | (-jz & 255), (jy << 8) | jz)
    key_ref[...] = ((index >> 16) << 16) | folded


def charge_kernel(
    count,
    place_ref,
    atoms_ref,
    spread_ref,
    coef_ref,
    radial_ref,
    inter_ref,
    index_ref,
    key_ref,
    order_ref,
    pot_ref,
    sent_ref,
    cos_ref,
    sin_ref,
    weights,
    rows_scratch,
    values,
):
    step = pl.program_id(0)
    atoms = atoms_ref.shape[0]
    per_chunk = CHUNK // 128

    @pl.when(step == 0)
    def _():
        kind = atoms_ref[:, LM + 3 : LM + 4]
        total = jnp.zeros((atoms, ROWS), F32)
        for s in range(KINDS):
            moved = jnp.dot(
                atoms_ref[...], spread_ref[s], precision=HIGH, preferred_element_type=F32
            )
            total = total + jnp.where(kind == float(s), moved, 0.0)
        high, low = split(total)
        weights[0:atoms, :] = high
        weights[atoms : 2 * atoms, :] = low

    jx, *freq = frequencies(index_ref[...], place_ref[0], count)
    table_high, table_low = table_of(freq, radial_ref, coef_ref, rows_scratch)
    main = jnp.dot(weights[...], table_high, preferred_element_type=F32)
    rest = jnp.dot(weights[0:atoms, :], table_low, preferred_element_type=F32)
    shape_part = main[0:atoms] + (main[atoms:] + rest)
    cosine, sine = angles(atoms_ref, freq)
    cos_ref[...] = cosine
    sin_ref[...] = sine
    pseudo_re = jnp.sum(shape_part * cosine, axis=0, keepdims=True)
    pseudo_im = -jnp.sum(shape_part * sine, axis=0, keepdims=True)
    freq_x, freq_y, freq_z = freq
    size_sq = freq_x * freq_x + freq_y * freq_y + freq_z * freq_z
    kernel = jnp.where(size_sq > 0, 1.0 / jnp.maximum(size_sq, 1.0), 0.0)
    pot_re = (inter_ref[0:1, :] + pseudo_re) * kernel
    pot_im = (inter_ref[1:2, :] + pseudo_im) * kernel
    pot_ref[0:1, :] = pot_re
    pot_ref[1:2, :] = pot_im
    folded_im = jnp.where(jx > NG // 2, -pot_im, pot_im)
    for j in range(per_chunk):
        line = pl.ds(step * per_chunk + j, 1)
        values[0, line, :] = pot_re[:, j * 128 : (j + 1) * 128]
        values[1, line, :] = folded_im[:, j * 128 : (j + 1) * 128]

    @pl.when(step == pl.num_programs(0) - 1)
    def _():
        order = order_ref[...]
        lines = order.shape[0]
        lane = order & 127
        line_of = order >> 7

        def one_line(r, carried):
            taken_re, taken_im = carried
            here = line_of == r
            row_re = jnp.broadcast_to(values[0, pl.ds(r, 1), :], (lines, 128))
            row_im = jnp.broadcast_to(values[1, pl.ds(r, 1), :], (lines, 128))
            taken_re = jnp.where(here, jnp.take_along_axis(row_re, lane, 1, mode="promise_in_bounds"), taken_re)
            taken_im = jnp.where(here, jnp.take_along_axis(row_im, lane, 1, mode="promise_in_bounds"), taken_im)
            return taken_re, taken_im

        empty = jnp.zeros((lines, 128), F32)
        taken_re, taken_im = lax.fori_loop(0, lines, one_line, (empty, empty), unroll=32)
        key = key_ref[...]
        sent_ref[0:lines, :] = taken_re
        sent_ref[lines : 2 * lines, :] = taken_im
        sent_ref[2 * lines : 3 * lines, :] = key.astype(F32)
        begins = (lax.broadcasted_iota(I32, (8, 128), 1) * 256).astype(F32)
        ends = begins + 255.0
        first = jnp.zeros((8, 128), F32)
        last = jnp.zeros((8, 128), F32)
        for k in range(1, NG // count):
            below = jnp.sum((key < (k << 16)).astype(F32), axis=(0, 1), keepdims=True)
            first = first + jnp.where(below <= begins, 1.0, 0.0)
            last = last + jnp.where(below <= ends, 1.0, 0.0)
        sub = lax.broadcasted_iota(I32, (8, 128), 0)
        sent_ref[3 * lines :, :] = jnp.where(sub == 0, first, last)


def boundary_kernel(
    count,
    place_ref,
    atoms_ref,
    gather_ref,
    coef_ref,
    slot_ref,
    bessel_ref,
    pot_ref,
    index_ref,
    cos_ref,
    sin_ref,
    out_ref,
    total,
    rows_scratch,
):
    step = pl.program_id(0)
    atoms = atoms_ref.shape[0]
    _, *freq = frequencies(index_ref[...], place_ref[0], count)
    table_high, table_low = table_of(freq, bessel_ref, coef_ref, rows_scratch)
    cosine, sine = cos_ref[...], sin_ref[...]
    pot_re, pot_im = pot_ref[0:1, :], pot_ref[1:2, :]
    real_part = pot_re * cosine - pot_im * sine
    imag_part = pot_re * sine + pot_im * cosine
    high, low = split(jnp.concatenate([real_part, imag_part], 0))
    dims = (((1,), (1,)), ((), ()))
    both = lax.dot_general(
        jnp.concatenate([high, low], 0), table_high, dims, preferred_element_type=F32
    )
    rest = lax.dot_general(high, table_low, dims, preferred_element_type=F32)
    add = both[0 : 2 * atoms] + (both[2 * atoms :] + rest)

    @pl.when(step == 0)
    def _():
        total[...] = add

    @pl.when(step > 0)
    def _():
        total[...] += add

    @pl.when(step == pl.num_programs(0) - 1)
    def _():
        kind = atoms_ref[:, LM + 3 : LM + 4]
        raw = jnp.zeros((atoms, 128), F32)
        for s in range(KINDS):
            part = jnp.dot(
                total[0:atoms, :], gather_ref[s], precision=HIGH, preferred_element_type=F32
            ) + jnp.dot(
                total[atoms:, :], gather_ref[KINDS + s], precision=HIGH, preferred_element_type=F32
            )
            raw = raw + jnp.where(kind == float(s), part, 0.0)
        slots = lax.broadcasted_iota(I32, (atoms, atoms), 0)
        moved = (slots == slot_ref[...]).astype(F32)
        out_ref[...] = jnp.dot(moved, raw, precision=HIGH, preferred_element_type=F32)


def plane_type(place):
    return ((place >> 1) ^ ((place & 1) * (place >> 2))) & 1


def planes_kernel(count, pattern, *refs):
    place_ref, recv_ref, step_ref, own_out, other_out = refs[:5]
    own_ref, other_ref, wave, start_ref, sem, store_sem = refs[5:11]
    box, front, back, fields = refs[11:]
    rows = NG // count
    chip_rows = 2 * rows
    sources = recv_ref.shape[0]
    lines = (recv_ref.shape[1] - 8) // 3
    halves = 1 if pattern is None else 2
    local_planes = NG // 4 // halves
    pitch = 2 * GROUP + 8
    tiles = lines // 2
    together = math.gcd(tiles, 16)
    place = place_ref[0]
    core = place % 2
    base = (place // 2) * chip_rows

    fetch = pltpu.make_async_copy(recv_ref.at[:, pl.ds(3 * lines, 8), :], start_ref, sem.at[0])
    fetch.start()
    box[...] = jnp.zeros_like(box)

    sub = lax.broadcasted_iota(I32, (8, 128), 0)
    if chip_rows == 8:
        start_rows = (base + (sub + core * rows) % chip_rows).astype(F32) * (1.0 / NG)
    else:
        start_rows = (base + core * rows + sub).astype(F32) * (1.0 / NG)
    across = (1 - 2 * core).astype(F32) * (rows / NG)

    def all_fields(s, _):
        keys = recv_ref[s, 2 * lines : 3 * lines, :].astype(I32)
        jy = ((keys >> 8) & 255).astype(F32)
        fields[s, 0] = jy
        fields[s, 1] = (keys & 255).astype(F32)
        fields[s, 2] = (keys >> 16).astype(F32)
        if chip_rows > 8:
            fields[s, 3], fields[s, 4] = turn(jy * (8.0 / NG))
            fields[s, 5], fields[s, 6] = turn(jy * across)
        return 0

    lax.fori_loop(0, sources, all_fields, 0)

    def one_chunk(s, i, held):
        v_re = recv_ref[s, pl.ds(i, 1), :]
        v_im = recv_ref[s, pl.ds(lines + i, 1), :]
        jy, c_step, s_step, c_far, s_far = (
            fields[s, f, pl.ds(i, 1), :] if f == 0 or chip_rows > 8 else None
            for f in (0, 3, 4, 5, 6)
        )
        c, s = turn(jnp.broadcast_to(jy, (8, 128)) * start_rows)
        parts = [(v_re * c - v_im * s, v_re * s + v_im * c)]
        if chip_rows > 8:
            while 8 * len(parts) < rows:
                re, im = parts[-1]
                parts.append((re * c_step - im * s_step, re * s_step + im * c_step))
            parts += [(re * c_far - im * s_far, re * s_far + im * c_far) for re, im in parts]
        high, low = split(jnp.concatenate([re for re, _ in parts] + [im for _, im in parts], 0))
        held[i] = jnp.concatenate([high, low], 0)

    def edge(s, t, which):
        return start_ref[s, which, t].astype(I32)

    def plane_at(s, k):
        if pattern is None:
            owner = 2 * s + core
        else:
            owner = place ^ pattern ^ (8 * (s >> 1) + (4 + 2 * core) * (s & 1))
        jx = k * count + owner
        return jnp.where(jx > NG // 2, NG - jx, jx) // (2 * halves)

    def add_tile(s, t, wanted, held):
        left, right = [], []
        for i in (2 * t, 2 * t + 1):
            spot = jnp.broadcast_to(fields[s, 1, pl.ds(i, 1), :], (16, 128)).astype(BF16)
            hits = [
                jnp.where(
                    step_ref[16 * r : 16 * r + 16, :] == spot,
                    jnp.ones((16, 128), BF16),
                    jnp.zeros((16, 128), BF16),
                )
                for r in range(NG // 16)
            ]
            right.append(jnp.concatenate(hits, 0))
            plane = jnp.broadcast_to(fields[s, 2, pl.ds(i, 1), :], (16, 128))
            phased = held[i]
            masked = []
            for k, used in wanted:
                mask = jnp.where(plane == k.astype(F32), used, 0.0).astype(BF16)
                masked.append(phased * jnp.concatenate([mask] * (phased.shape[0] // 16), 0))
            left.append(jnp.concatenate(masked, 0))
        out = lax.dot_general(
            jnp.concatenate(left, 1),
            jnp.concatenate(right, 1),
            (((1,), (1,)), ((), ())),
            preferred_element_type=F32,
        )
        size = 2 * chip_rows
        for j, (k, _) in enumerate(wanted):
            box[plane_at(s, k)] += (
                out[2 * j * size : (2 * j + 1) * size] + out[(2 * j + 1) * size : (2 * j + 2) * size]
            )

    def one_source(s, held, following, filled):
        def some_tiles(g, most):
            for j in range(together):
                t = g * together + j
                first, last = edge(s, t, 0), edge(s, t, 1)
                second = jnp.where(last > first, 1.0, 0.0)
                add_tile(s, t, [(first, 1.0), (last, second)], held)
                if filled is not None:
                    one_chunk(following, 2 * t, filled)
                    one_chunk(following, 2 * t + 1, filled)
                most = jnp.maximum(most, last - first)
            return most

        most = lax.fori_loop(0, tiles // together, some_tiles, jnp.int32(0))

        @pl.when(most > 1)
        def _():
            def one_tile(t, _):
                def between(k, _):
                    add_tile(s, t, [(k, 1.0)], held)
                    return 0

                return lax.fori_loop(edge(s, t, 0) + 1, edge(s, t, 1), between, 0)

            lax.fori_loop(0, tiles, one_tile, 0)

    def first_chunks(g, _):
        for j in range(8):
            one_chunk(0, 8 * g + j, front)
        return 0

    lax.fori_loop(0, lines // 8, first_chunks, 0)
    fetch.wait()

    def two_sources(t, _):
        one_source(2 * t, front, 2 * t + 1, back)
        one_source(2 * t + 1, back, 2 * t + 2, front)
        return 0

    lax.fori_loop(0, sources // 2 - 1, two_sources, 0)
    one_source(sources - 2, front, sources - 1, back)
    one_source(sources - 1, back, None, None)
    grid = [lax.broadcasted_iota(I32, (NG, NG), d).astype(F32) for d in range(2)]
    cos_z, sin_z = turn(grid[0] * grid[1] * (1.0 / NG))
    for j, table in enumerate(([cos_z, sin_z], [-sin_z, cos_z])):
        high, low = split(jnp.concatenate(table, 1))
        for k, part in enumerate((high, high, low)):
            wave[(3 * j + k) * NG : (3 * j + k + 1) * NG, :] = part

    def along_z(at, number):
        block = box[pl.ds(at, number)]
        left = []
        for part in (block[:, :chip_rows], block[:, chip_rows:]):
            high, low = split(part.reshape(number * chip_rows, NG))
            left += [high, low, high]
        out = jnp.dot(jnp.concatenate(left, 1), wave[...], preferred_element_type=F32)
        out = out.reshape(number, chip_rows, 2 * NG)
        return out[:, :, :NG], out[:, :, NG:]

    def keep(g, at, value):
        line = pl.ds(at, rows, stride=pitch)
        for h in range(2):
            own_ref[g, h, line, :] = value[:rows, h * 128 : (h + 1) * 128]
            other_ref[g, h, line, :] = value[rows:, h * 128 : (h + 1) * 128]

    has_middle = core == 0
    if pattern is not None:
        has_middle = has_middle & (plane_type(place) == (1 if pattern else 0))
    stores = []
    for g in range(local_planes // GROUP):
        re, im = along_z(g * GROUP, GROUP)
        for j in range(GROUP):
            keep(g, 2 * j, re[j])
            keep(g, 2 * j + 1, im[j])
        if g == 0:

            @pl.when(has_middle)
            def _():
                re, _ = along_z(local_planes, 1)
                keep(0, 1, re[0])

        for j, (made, out) in enumerate(((other_ref, other_out), (own_ref, own_out))):
            stores.append(pltpu.make_async_copy(made.at[g], out.at[g], store_sem.at[g, j]))
            stores[-1].start()
    for store in stores:
        store.wait()


def planes_call(count, place, recv, pattern, steps):
    rows = NG // count
    sources = recv.shape[0]
    lines = (recv.shape[1] - 8) // 3
    local_planes = NG // 4 // (1 if pattern is None else 2)
    groups = local_planes // GROUP
    half = jax.ShapeDtypeStruct((groups, 2, rows * (2 * GROUP + 8), 128), F32)
    vmem = pl.BlockSpec(memory_space=pltpu.VMEM)
    anywhere = pl.BlockSpec(memory_space=pltpu.HBM)
    held = pltpu.VMEM((lines, 8 * rows, 128), BF16)
    return pl.pallas_call(
        functools.partial(planes_kernel, count, pattern),
        in_specs=[smem(), vmem, vmem],
        out_specs=[anywhere, anywhere],
        out_shape=[half, half],
        scratch_shapes=[
            pltpu.VMEM(half.shape, F32),
            pltpu.VMEM(half.shape, F32),
            pltpu.VMEM((6 * NG, 2 * NG), BF16),
            pltpu.SMEM((sources, 8, 128), F32),
            pltpu.SemaphoreType.DMA((2,)),
            pltpu.SemaphoreType.DMA((groups, 2)),
            pltpu.VMEM((local_planes + 1, 4 * rows, NG), F32),
            held,
            held,
            pltpu.VMEM((sources, 7, lines, 128), F32),
        ],
        compiler_params=params(PLANES_MB),
        name="planes_far" if pattern else "planes_near",
        cost_estimate=cost(15),
    )(place, recv, steps)


def last_kernel(count, place_ref, wave_ref, *refs):
    halves = (len(refs) - 6) // 2
    given = refs[: 2 * halves]
    out_ref, held, wave, tables_ref, parts, sem = refs[2 * halves :]
    rows = NG // count
    pitch = 2 * GROUP + 8
    place = place_ref[0]
    group = 4
    fetch_tables = pltpu.make_async_copy(wave_ref, tables_ref, sem.at[0, 2 * halves])
    fetch_tables.start()
    fetches = []
    for g in range(rows // group):
        line = pl.ds(g * group * pitch, group * pitch)
        fetches.append(
            [
                pltpu.make_async_copy(
                    part.at[:, :, line, :], parts.at[i, :, :, line, :], sem.at[g, i]
                )
                for i, part in enumerate(given)
            ]
        )
        for fetch in fetches[-1]:
            fetch.start()
    fetch_tables.wait()
    tables = []
    for device in (place, place ^ 1):
        for half in range(halves):
            which = device & 1
            if halves == 2:
                which = 2 * which + (plane_type(device) ^ half)
            tables.append(tables_ref[which])
    wave[0], wave[1] = split(jnp.concatenate(tables, 0).T)

    def one_row(y):
        line = pl.ds(y * pitch, 2 * GROUP)
        mixed = [
            jnp.concatenate(
                [parts[i, q, h, line, :] for i in range(2 * halves) for q in range(parts.shape[1])],
                0,
            )
            for h in range(2)
        ]
        high, low = split(jnp.concatenate(mixed, 1))
        main = jnp.dot(wave[...].reshape(2 * NG, NG), high, preferred_element_type=F32)
        rest = jnp.dot(wave[0], low, preferred_element_type=F32)
        out = main[:NG] + (main[NG:] + rest)
        for h in range(2):
            held[h, pl.ds(y, NG, stride=rows), :] = out[:, h * 128 : (h + 1) * 128]

    for g in range(rows // group):
        for fetch in fetches[g]:
            fetch.wait()
        for y in range(g * group, (g + 1) * group):
            one_row(y)
    copies = [
        pltpu.make_async_copy(held.at[h], out_ref.at[:, pl.ds(h * 128, 128)], sem.at[0, h])
        for h in range(2)
    ]
    for copy in copies:
        copy.start()
    for copy in copies:
        copy.wait()


def wave_tables(halves):
    j = np.arange(NG)
    along_x = []
    for core in range(2):
        for kind in range(halves):
            planes = np.arange(core, NG // 2, 2)
            if halves == 2 and core == 0:
                planes = planes[planes % 4 == 2 * kind]
            elif halves == 2:
                planes = planes[np.isin(planes % 8, (3, 5) if kind else (1, 7))]
            phase = 2 * np.pi / NG * ((planes[:, None] * j[None, :]) % NG)
            table = np.stack([np.cos(phase), -np.sin(phase)], 1).reshape(-1, NG)
            if planes[0] == 0:
                table[1] = np.cos(np.pi * j)
            along_x.append(table)
    return np.stack(along_x).astype(np.float32)


def smem():
    return pl.BlockSpec(memory_space=pltpu.SMEM)


def cost(micros):
    return pl.CostEstimate(flops=int(micros * 1e9), bytes_accessed=0, transcendentals=0)


def params(megabytes=56):
    return pltpu.CompilerParams(vmem_limit_bytes=megabytes * 1024 * 1024)


def body(
    multipoles, positions, species, atom_slot, pseudo_radial, boundary_bessel, interstitial, g_index
):
    count = lax.axis_size("pencil")
    owner = lax.axis_index("pencil").astype(I32)
    place = owner.reshape(1)
    local_g = g_index.shape[0]
    lines = local_g // 128
    chunks = local_g // CHUNK
    atoms = atom_slot.shape[0]
    own_atoms = multipoles.shape[1]
    rows = NG // count
    spread, gather = placement_tables()
    coef = jnp.asarray(recurrence_table())
    along_x = wave_tables(2 if count == 16 else 1)

    vmem = pl.BlockSpec(memory_space=pltpu.VMEM)
    copies, key = pl.pallas_call(
        functools.partial(gather_kernel, count),
        in_specs=[smem(), vmem, vmem, vmem, vmem],
        out_specs=[vmem, vmem],
        out_shape=[
            jax.ShapeDtypeStruct((count, own_atoms, 128), F32),
            jax.ShapeDtypeStruct((lines, 128), I32),
        ],
        scratch_shapes=[pltpu.VMEM((own_atoms, 128), F32)],
        compiler_params=params(),
        name="atoms",
    )(
        place,
        multipoles.T,
        positions,
        species.reshape(1, own_atoms),
        g_index.reshape(lines, 128),
    )
    atom_rows = lax.all_to_all(copies, "pencil", split_axis=0, concat_axis=0, tiled=True)
    atom_rows = atom_rows.reshape(atoms, 128)

    key, order = lax.sort(
        (key.reshape(local_g), lax.iota(I32, local_g)), num_keys=1, is_stable=False
    )
    key = key.reshape(lines, 128)
    order = order.reshape(lines, 128)
    index_line = g_index.reshape(1, local_g)

    whole = lambda a: pl.BlockSpec(a.shape, lambda i: (0,) * a.ndim)
    line_spec = pl.BlockSpec((1, CHUNK), lambda i: (0, i))
    pair_spec = pl.BlockSpec((2, CHUNK), lambda i: (0, i))
    radial_spec = pl.BlockSpec((LMAX + 1, KINDS, CHUNK), lambda i: (0, 0, i))
    spread = jnp.asarray(spread)
    atom_spec = pl.BlockSpec((atoms, CHUNK), lambda i: (0, i))
    pot, sent, cosine, sine = pl.pallas_call(
        functools.partial(charge_kernel, count),
        grid=(chunks,),
        in_specs=[
            smem(),
            whole(atom_rows),
            whole(spread),
            whole(coef),
            radial_spec,
            pair_spec,
            line_spec,
            whole(key),
            whole(order),
        ],
        out_specs=[
            pair_spec,
            pl.BlockSpec((3 * lines + 8, 128), lambda i: (0, 0)),
            atom_spec,
            atom_spec,
        ],
        out_shape=[
            jax.ShapeDtypeStruct((2, local_g), F32),
            jax.ShapeDtypeStruct((3 * lines + 8, 128), F32),
            jax.ShapeDtypeStruct((atoms, local_g), F32),
            jax.ShapeDtypeStruct((atoms, local_g), F32),
        ],
        scratch_shapes=[
            pltpu.VMEM((2 * atoms, ROWS), BF16),
            pltpu.VMEM((8, 8, CHUNK), F32),
            pltpu.VMEM((2, lines, 128), F32),
        ],
        compiler_params=params(),
        name="charge",
        cost_estimate=cost(10),
    )(place, atom_rows, spread, coef, pseudo_radial.transpose(1, 0, 2), interstitial, index_line, key, order)

    gather = jnp.asarray(gather)
    slot_line = atom_slot.reshape(1, atoms)
    partial_raw = pl.pallas_call(
        functools.partial(boundary_kernel, count),
        grid=(chunks,),
        in_specs=[
            smem(),
            whole(atom_rows),
            whole(gather),
            whole(coef),
            whole(slot_line),
            radial_spec,
            pair_spec,
            line_spec,
            atom_spec,
            atom_spec,
        ],
        out_specs=pl.BlockSpec((atoms, 128), lambda i: (0, 0)),
        out_shape=jax.ShapeDtypeStruct((atoms, 128), F32),
        scratch_shapes=[
            pltpu.VMEM((2 * atoms, ROWS), F32),
            pltpu.VMEM((8, 8, CHUNK), F32),
        ],
        compiler_params=params(),
        name="boundary",
        cost_estimate=cost(10),
    )(place, atom_rows, gather, coef, slot_line, boundary_bessel.transpose(1, 0, 2), pot, index_line, cosine, sine)
    parts = lax.all_to_all(partial_raw, "pencil", split_axis=0, concat_axis=0, tiled=True)

    steps = jnp.asarray(np.broadcast_to(np.arange(NG)[:, None], (NG, 128)).astype(BF16))
    sibling = [(i, i ^ 1) for i in range(count)]
    if count == 16:
        masks = [lambda i: 4 + 2 * (i & 1), lambda i: 8, lambda i: 12 + 2 * (i & 1)]
        pieces = [
            lax.ppermute(sent, "pencil", [(i, i ^ mask(i)) for i in range(count)])
            for mask in masks
        ]
        pieces, partial_raw = lax.optimization_barrier((pieces, partial_raw))
        near = jnp.stack([sent] + pieces)
        far = lax.ppermute(near, "pencil", [(i, i ^ 2) for i in range(count)])
        own_near, other_near = planes_call(count, place, near, 0, steps)
        other_near = lax.ppermute(other_near, "pencil", sibling)
        far, parts = lax.optimization_barrier((far, parts))
        own_far, other_far = planes_call(count, place, far, 2, steps)
        other_far = lax.ppermute(other_far, "pencil", sibling)
        waves = [own_near, own_far, other_near, other_far]
    else:
        groups = [list(range(c, count, 2)) for c in range(2)]
        recv = lax.all_gather(sent, "pencil", axis_index_groups=groups)
        own, other = planes_call(count, place, recv, None, steps)
        waves = [own, lax.ppermute(other, "pencil", sibling)]

    boundary = jnp.sum(parts.reshape(count, own_atoms, 128), axis=0)[:, :LM].T
    along_x = jnp.asarray(along_x)
    anywhere = pl.BlockSpec(memory_space=pltpu.HBM)
    potential = pl.pallas_call(
        functools.partial(last_kernel, count),
        in_specs=[smem()] + [anywhere] * (1 + len(waves)),
        out_specs=anywhere,
        out_shape=jax.ShapeDtypeStruct((NG * rows, NG), F32),
        scratch_shapes=[
            pltpu.VMEM((2, NG * rows, 128), F32),
            pltpu.VMEM((2, NG, NG), BF16),
            pltpu.VMEM(along_x.shape, F32),
            pltpu.VMEM((len(waves),) + waves[0].shape, F32),
            pltpu.SemaphoreType.DMA((rows // 4, 5)),
        ],
        compiler_params=params(LAST_MB),
        name="last",
        cost_estimate=cost(7),
    )(place, along_x, *waves)
    return (potential.reshape(NG, rows, NG), boundary)


def solution(mesh):
    placed = (
        P(None, ("cells", "pencil")),
        P(None, ("cells", "pencil")),
        P(("cells", "pencil")),
        P("cells"),
        P(None, None, ("cells", "pencil")),
        P(None, None, ("cells", "pencil")),
        P(None, ("cells", "pencil")),
        P(("cells", "pencil")),
    )
    return jax.shard_map(
        body,
        mesh=mesh,
        in_specs=placed,
        out_specs=(P("cells", "pencil", None), P(None, ("cells", "pencil"))),
        check_vma=False,
    )
```
